32 devices in a mesh: clip: 4 (over x, core), ctx: 2 (over y), tp: 4 (over z).
Axes of the slice: x: 2, y: 2, z: 4, core: 2. Of those that a mesh axis runs over, the one named last changes fastest.
Arguments:
- frames: bfloat16 [4096, 768], P(('clip', 'ctx')), may hold values from -6 to 6
- cotangent: bfloat16 [4096, 768], P(('clip', 'ctx')), may hold values from -6 to 6
- first_gain: bfloat16 [768], P('clip'), may hold values from 0.099609375 to 1.8984375
- first_shift: bfloat16 [768], P('clip'), may hold values from -3 to 3
- query_weight: bfloat16 [768, 768], P('clip', 'tp'), may hold values from -0.21875 to 0.21875
- query_bias: bfloat16 [768], P('tp'), may hold values from -3 to 3
- key_weight: bfloat16 [768, 768], P('clip', 'tp'), may hold values from -0.21875 to 0.21875
- value_weight: bfloat16 [768, 768], P('clip', 'tp'), may hold values from -0.21875 to 0.21875
- value_bias: bfloat16 [768], P('tp'), may hold values from -3 to 3
- out_weight: bfloat16 [768, 768], P('tp', 'clip'), may hold values from -1.75 to 1.75
- out_bias: bfloat16 [768], P('clip'), may hold values from -3 to 3
- second_gain: bfloat16 [768], P('clip'), may hold values from 0.099609375 to 1.8984375
- second_shift: bfloat16 [768], P('clip'), may hold values from -3 to 3
- expand_weight: bfloat16 [768, 3072], P('clip', 'tp'), may hold values from -0.21875 to 0.21875
- expand_bias: bfloat16 [3072], P('tp'), may hold values from -3 to 3
- reduce_weight: bfloat16 [3072, 768], P('tp', 'clip'), may hold values from -0.109375 to 0.109375
- reduce_bias: bfloat16 [768], P('clip'), may hold values from -3 to 3
Outputs:
- layer_out: bfloat16 [4096, 768], P(('clip', 'ctx'))
- frames_grad: float32 [4096, 768], P(('clip', 'ctx'))
- first_gain_grad: float32 [768], P('clip')
- first_shift_grad: float32 [768], P('clip')
- query_weight_grad: float32 [768, 768], P('clip', 'tp')
- query_bias_grad: float32 [768], P('tp')
- key_weight_grad: float32 [768, 768], P('clip', 'tp')
- value_weight_grad: float32 [768, 768], P('clip', 'tp')
- value_bias_grad: float32 [768], P('tp')
- out_weight_grad: float32 [768, 768], P('tp', 'clip')
- out_bias_grad: float32 [768], P('clip')
- second_gain_grad: float32 [768], P('clip')
- second_shift_grad: float32 [768], P('clip')
- expand_weight_grad: float32 [768, 3072], P('clip', 'tp')
- expand_bias_grad: float32 [3072], P('tp')
- reduce_weight_grad: float32 [3072, 768], P('tp', 'clip')
- reduce_bias_grad: float32 [768], P('clip')
The draws below stay inside these ranges and needn't reach their ends.
All inputs are finite; a program needn't handle non-finite values.
Results may differ from the reference program's by a relative error of at most 0.023.
Values may be sent and summed in bfloat16 or wider, within the bound.
A program may use at most 128 MiB of HBM per device.

```python
import math
import jax
import jax.numpy as jnp
from jax import lax

D = 768
H = 12
DH = 64
FF = 3072
FRAMES = 1024
CLIPS = 4
TOKENS = 4096


def block_scale(key, shape, cuts, smallest, largest):
    level = 1.0
    for axis_at, blocks in cuts:
        draws = jax.random.uniform(jax.random.fold_in(jax.random.fold_in(key, 6), axis_at), (blocks,), jnp.float32, smallest / len(cuts), largest / len(cuts))
        level = level * jnp.repeat(jnp.exp(draws), shape[axis_at] // blocks).reshape((-1,) + (1,) * (len(shape) - 1 - axis_at))
    return level


def normal_values(rng, shape, scale, limit, pieces=(), held_as=jnp.bfloat16):
    values = jax.random.normal(rng, shape, jnp.float32) * scale
    if len(pieces) > 0:
        values = block_scale(rng, shape, pieces, -0.22, 0.18) * values
    return jnp.clip(values, min=-limit, max=limit).astype(held_as)


def setup_inputs(seed: int = 0) -> dict:
    streams_of = jax.random.split(jax.random.key(seed), 18)
    return {
        "frames": normal_values(streams_of[0], (TOKENS, D), 1.0, 6.0, ((0, 8),)),
        "cotangent": normal_values(streams_of[1], (TOKENS, D), 1.0, 6.0, ((0, 8),)),
        "first_gain": jnp.clip(1.0 + 0.18 * jax.random.normal(streams_of[2], (D,), jnp.float32), 0.099609375, 1.8984375).astype(jnp.bfloat16),
        "first_shift": normal_values(streams_of[3], (D,), 0.5, 3.0, ((0, 4),)),
        "query_weight": normal_values(streams_of[4], (D, D), D ** -0.5, 0.21875, ((0, 4), (1, 4))),
        "query_bias": normal_values(streams_of[5], (D,), 0.5, 3.0, ((0, 4),)),
        "key_weight": normal_values(streams_of[6], (D, D), D ** -0.5, 0.21875, ((0, 4), (1, 4))),
        "value_weight": normal_values(streams_of[7], (D, D), D ** -0.5, 0.21875, ((0, 4), (1, 4))),
        "value_bias": normal_values(streams_of[8], (D,), 0.5, 3.0, ((0, 4),)),
        "out_weight": normal_values(streams_of[9], (D, D), (max(1, D * 16 // FRAMES)) ** -0.5, 1.75, ((0, 4), (1, 4))),
        "out_bias": normal_values(streams_of[10], (D,), 0.5, 3.0, ((0, 4),)),
        "second_gain": jnp.clip(1.0 + 0.18 * jax.random.normal(streams_of[11], (D,), jnp.float32), 0.099609375, 1.8984375).astype(jnp.bfloat16),
        "second_shift": normal_values(streams_of[12], (D,), 0.5, 3.0, ((0, 4),)),
        "expand_weight": normal_values(streams_of[13], (D, FF), D ** -0.5, 0.21875, ((0, 4), (1, 4))),
        "expand_bias": normal_values(streams_of[14], (FF,), 0.5, 3.0, ((0, 4),)),
        "reduce_weight": normal_values(streams_of[15], (FF, D), FF ** -0.5, 0.109375, ((0, 4), (1, 4))),
        "reduce_bias": normal_values(streams_of[16], (D,), 0.5, 3.0, ((0, 4),)),
    }


@jax.custom_vjp
def low(v):
    return lax.optimization_barrier(v.astype(jnp.bfloat16)).astype(jnp.float32)

@jax.custom_vjp
def low_back(v):
    return v

def low_keep(v):
    return (low(v), None)

def low_pass(kept, grad):
    return (grad,)

def back_keep(v):
    return (v, None)

def back_low(kept, grad):
    return (low(grad),)
low.defvjp(low_keep, low_pass)
low_back.defvjp(back_keep, back_low)

def matmul(left, right):
    return jnp.dot(left, right, precision=lax.Precision.HIGHEST, preferred_element_type=jnp.float32)

def layer_norm(matrix, gain, shift):
    row_mean = lax.optimization_barrier(jnp.mean(matrix, axis=-1, keepdims=True))
    centred = matrix - row_mean
    spread = lax.optimization_barrier(jnp.mean(centred * centred, axis=-1, keepdims=True))
    return centred * lax.rsqrt(spread + 1e-05) * gain + shift

def attend_block(query_block, key_clip, value_clip):
    scores = jnp.einsum('qhd,khd->hqk', query_block, key_clip, precision=lax.Precision.HIGHEST)
    scores = low_back(scores * DH ** (-0.5))
    weights = low(jax.nn.softmax(scores, axis=-1))
    return jnp.einsum('hqk,khd->qhd', weights, value_clip, precision=lax.Precision.HIGHEST)

def attend_clip(triple):
    query_clip, key_clip, value_clip = triple
    block = math.gcd(FRAMES, 512)
    blocks = query_clip.reshape(FRAMES // block, block, H, DH)

    def one_block(query_block):
        return attend_block(query_block, key_clip, value_clip)
    return lax.map(jax.checkpoint(one_block), blocks).reshape(FRAMES, H, DH)

def forward(frames, first_gain, first_shift, query_weight, query_bias, key_weight, value_weight, value_bias, out_weight, out_bias, second_gain, second_shift, expand_weight, expand_bias, reduce_weight, reduce_bias):
    first_norm = low(layer_norm(frames, first_gain, first_shift))
    queries = low(low_back(matmul(first_norm, query_weight) + query_bias))
    keys = low(low_back(matmul(first_norm, key_weight)))
    values = low(low_back(matmul(first_norm, value_weight) + value_bias))
    shape = (CLIPS, FRAMES, H, DH)
    mixed = lax.map(attend_clip, (queries.reshape(shape), keys.reshape(shape), values.reshape(shape)))
    mixed = low(low_back(mixed.reshape(TOKENS, D)))
    hidden = frames + low_back(matmul(mixed, out_weight) + out_bias)
    second_norm = low(layer_norm(hidden, second_gain, second_shift))
    pre_act = low_back(matmul(second_norm, expand_weight) + expand_bias)
    activated = low(jax.nn.gelu(pre_act, approximate=False))
    return hidden + low_back(matmul(activated, reduce_weight) + reduce_bias)

def reference(frames, cotangent, first_gain, first_shift, query_weight, query_bias, key_weight, value_weight, value_bias, out_weight, out_bias, second_gain, second_shift, expand_weight, expand_bias, reduce_weight, reduce_bias):
    inputs = [frames, first_gain, first_shift, query_weight, query_bias, key_weight, value_weight, value_bias, out_weight, out_bias, second_gain, second_shift, expand_weight, expand_bias, reduce_weight, reduce_bias]
    inputs = [item.astype(jnp.float32) for item in inputs]
    result, pullback = jax.vjp(forward, *inputs)
    grads = pullback(cotangent.astype(jnp.float32))
    return (result.astype(jnp.bfloat16), grads[0], grads[1], grads[2], grads[3], grads[4], grads[5], grads[6], grads[7], grads[8], grads[9], grads[10], grads[11], grads[12], grads[13], grads[14], grads[15])
```

```python
import functools
import itertools

import jax
import jax.numpy as jnp
from jax import lax
from jax.experimental import pallas as pl
from jax.experimental.pallas import tpu as pltpu
from jax.sharding import PartitionSpec as P

DH = 64


def center_rows(matrix):
    row_mean = jnp.mean(matrix, axis=-1, keepdims=True)
    centred = matrix - row_mean
    factor = lax.rsqrt(jnp.mean(centred * centred, axis=-1, keepdims=True) + 1e-05)
    return (centred * factor, factor)


def norm_back(grad_norm, normed, factor, gain):
    grad_hat = grad_norm * gain
    inner = jnp.mean(grad_hat, axis=-1, keepdims=True)
    cross = jnp.mean(grad_hat * normed, axis=-1, keepdims=True)
    return factor * (grad_hat - inner - normed * cross)


def product(left, right):
    return jnp.dot(left, right, preferred_element_type=jnp.float32)


def rows_inner(left, right):
    return lax.dot_general(
        left, right, (((0,), (0,)), ((), ())), preferred_element_type=jnp.float32
    )


def cols_inner(left, right):
    return lax.dot_general(
        left, right, (((1,), (1,)), ((), ())), preferred_element_type=jnp.float32
    )


def score_block(query_heads, key_heads, value_heads, grad_heads, log_total, row_delta, score_scale):
    scores = (
        jnp.einsum("qhd,khd->qhk", query_heads, key_heads, preferred_element_type=jnp.float32)
        * score_scale
    )
    weights = jnp.exp(scores - log_total[..., None])
    grad_weights = jnp.einsum(
        "qhd,khd->qhk", grad_heads, value_heads, preferred_element_type=jnp.float32
    )
    grad_scores = (weights * (grad_weights - row_delta[..., None])).astype(jnp.bfloat16)
    return (weights.astype(jnp.bfloat16), grad_scores)


F32 = jnp.float32
BF16 = jnp.bfloat16


def offsets(sizes):
    return [o for o in itertools.product(*(range(s) for s in sizes)) if any(o)]


def group_place(axes, sizes, offset):
    index = 0
    place = {}
    for axis, size, step in zip(axes, sizes, offset):
        at = lax.rem(lax.axis_index(axis) + step, size)
        place[axis] = at
        index = index * size + at
    return place, index


def rows_at(index, rows):
    return pl.ds(pl.multiple_of(index * rows, rows), rows)


def send(src, dst, sems, slot, place):
    copy = pltpu.make_async_remote_copy(
        src_ref=src,
        dst_ref=dst,
        send_sem=sems.at[0, slot],
        recv_sem=sems.at[1, slot],
        device_id=place,
        device_id_type=pl.DeviceIdType.MESH,
    )
    copy.start()
    return copy


def finish(copies):
    for copy in copies:
        copy.wait_send()


def spread(src, dst, rows, axes, sizes, sems):
    _, mine = group_place(axes, sizes, (0,) * len(axes))
    copies = []
    for slot, offset in enumerate(offsets(sizes)):
        place, _ = group_place(axes, sizes, offset)
        copies.append(send(src, dst.at[rows_at(mine, rows)], sems, slot, place))
    return mine, copies


def deal(src, landing, rows, axes, sizes, sems):
    copies = []
    for slot, offset in enumerate(offsets(sizes)):
        place, theirs = group_place(axes, sizes, offset)
        copies.append(send(src.at[rows_at(theirs, rows)], landing.at[slot], sems, slot, place))
    _, mine = group_place(axes, sizes, (0,) * len(axes))
    return mine, copies


def gather_steps(axes, sizes, src, out, sems):
    rows = src.shape[0]
    mine, copies = spread(src, out, rows, axes, sizes, sems)
    out[rows_at(mine, rows), :] = src[...]
    yield
    for copy in copies:
        copy.wait_recv()
    finish(copies)


def scatter_steps(axes, sizes, src, out, landing, sems):
    rows = out.shape[0]
    mine, copies = deal(src, landing, rows, axes, sizes, sems)
    yield
    total = src[rows_at(mine, rows), :].astype(F32)
    for slot, copy in enumerate(copies):
        copy.wait_recv()
        total = total + landing[slot].astype(F32)
    out[...] = total.astype(out.dtype)
    finish(copies)


def reduce_steps(axes, sizes, src, out, landing, sems, back_sems):
    rows = landing.shape[1]
    mine, copies = deal(src, landing, rows, axes, sizes, sems)
    yield
    total = src[rows_at(mine, rows), :].astype(F32)
    for slot, copy in enumerate(copies):
        copy.wait_recv()
        total = total + landing[slot].astype(F32)
    block = rows_at(mine, rows)
    out[block, :] = total.astype(out.dtype)
    _, backs = spread(out.at[block], out, rows, axes, sizes, back_sems)
    yield
    for copy in backs:
        copy.wait_recv()
    finish(copies)
    finish(backs)


def sum_blocks(held, rows, count):
    total = held[0:rows, :].astype(F32)
    for index in range(1, count):
        total = total + held[index * rows : (index + 1) * rows, :].astype(F32)
    return total


def share_steps(axes, sizes, src, out, held, sems):
    rows = src.shape[0]
    mine, copies = spread(src, held, rows, axes, sizes, sems)
    held[rows_at(mine, rows), :] = src[...]
    yield
    for copy in copies:
        copy.wait_recv()
    out[...] = sum_blocks(held, rows, len(copies) + 1).astype(out.dtype)
    finish(copies)


def both_steps(axes, sizes, more_axes, more_sizes, src, out, landing, part, held, sems, more_sems):
    rows = out.shape[0]
    mine, copies = deal(src, landing, rows, axes, sizes, sems)
    yield
    total = src[rows_at(mine, rows), :].astype(F32)
    for slot, copy in enumerate(copies):
        copy.wait_recv()
        total = total + landing[slot].astype(F32)
    part[...] = total.astype(part.dtype)
    at, mores = spread(part, held, rows, more_axes, more_sizes, more_sems)
    held[rows_at(at, rows), :] = part[...]
    yield
    for copy in mores:
        copy.wait_recv()
    out[...] = sum_blocks(held, rows, len(mores) + 1).astype(out.dtype)
    finish(copies)
    finish(mores)


def plan_of(kind, axes, sizes, more, array, out_type):
    rows, cols = array.shape
    count = 1
    for size in sizes:
        count *= size
    peers = count - 1
    pair = pltpu.SemaphoreType.DMA((2, peers))
    if kind == "gather":
        return (count * rows, cols), [pair], functools.partial(gather_steps, axes, sizes)
    if kind == "share":
        held = pltpu.VMEM((count * rows, cols), array.dtype)
        return (rows, cols), [held, pair], functools.partial(share_steps, axes, sizes)
    block = rows // count
    landing = pltpu.VMEM((peers, block, cols), array.dtype)
    if kind == "scatter":
        return (block, cols), [landing, pair], functools.partial(scatter_steps, axes, sizes)
    if kind == "reduce":
        return (
            (rows, cols),
            [landing, pair, pair],
            functools.partial(reduce_steps, axes, sizes),
        )
    more_axes, more_sizes = more
    more_count = 1
    for size in more_sizes:
        more_count *= size
    return (
        (block, cols),
        [
            landing,
            pltpu.VMEM((block, cols), array.dtype),
            pltpu.VMEM((more_count * block, cols), array.dtype),
            pair,
            pltpu.SemaphoreType.DMA((2, more_count - 1)),
        ],
        functools.partial(both_steps, axes, sizes, more_axes, more_sizes),
    )


def transfers(collective_id, name, jobs):
    def sized(axes):
        return tuple(lax.axis_size(axis) for axis in axes)

    plans = []
    groups = []
    for job in jobs:
        kind, axes, array, out_type = job[:4]
        more = (job[4], sized(job[4])) if len(job) > 4 else None
        plans.append(plan_of(kind, axes, sized(axes), more, array, out_type))
        for group in (axes,) + ((job[4],) if len(job) > 4 else ()):
            if group not in groups:
                groups.append(group)
    places = {}
    for group in groups:
        for offset in offsets(sized(group)):
            key = tuple(sorted((a, o) for a, o in zip(group, offset) if o))
            places.setdefault(key, (group, offset))
    count = len(jobs)

    def kernel(*refs):
        sources, outs = refs[:count], refs[count : 2 * count]
        scratch = list(refs[2 * count :])
        barrier = pltpu.get_barrier_semaphore()
        for group, offset in places.values():
            place, _ = group_place(group, sized(group), offset)
            pl.semaphore_signal(
                barrier, inc=1, device_id=place, device_id_type=pl.DeviceIdType.MESH
            )
        pl.semaphore_wait(barrier, len(places))
        running = []
        for source, out, (_, needs, steps) in zip(sources, outs, plans):
            mine, scratch = scratch[: len(needs)], scratch[len(needs) :]
            running.append(steps(source, out, *mine))
        while running:
            running = [step for step in running if next(step, "end") != "end"]

    whole = pl.BlockSpec(memory_space=pltpu.VMEM)
    return pl.pallas_call(
        kernel,
        name=name,
        out_shape=[
            jax.ShapeDtypeStruct(plan[0], job[3]) for plan, job in zip(plans, jobs)
        ],
        in_specs=[whole] * count,
        out_specs=[whole] * count,
        scratch_shapes=[need for plan in plans for need in plan[1]],
        compiler_params=pltpu.CompilerParams(
            collective_id=collective_id,
            has_side_effects=True,
            vmem_limit_bytes=56 * 1024 * 1024,
        ),
    )(*[job[2] for job in jobs])


def pack_vectors(vectors):
    flat = jnp.concatenate(vectors)
    width = -(-flat.shape[0] // (8 * 128)) * 128
    return jnp.pad(flat, (0, 8 * width - flat.shape[0])).reshape(8, width)


def unpack_vectors(packed, sizes):
    flat = packed.reshape(-1)
    out = []
    at = 0
    for size in sizes:
        out.append(flat[at : at + size])
        at += size
    return out


def shards(
    frames,
    cotangent,
    first_gain,
    first_shift,
    query_weight,
    query_bias,
    key_weight,
    value_weight,
    value_bias,
    out_weight,
    out_bias,
    second_gain,
    second_shift,
    expand_weight,
    expand_bias,
    reduce_weight,
    reduce_bias,
):
    row_count, width = frames.shape
    local_width = query_weight.shape[1]
    head_count = local_width // DH
    score_scale = DH ** (-0.5)
    share = first_gain.shape[0]
    hidden_width = expand_weight.shape[1]
    clips = lax.axis_size("clip")
    clip_at = lax.axis_index("clip") * share
    wide = -(-share // 128) * 128
    vectors = jnp.pad(
        jnp.stack([first_gain, first_shift, out_bias, second_gain, second_shift, reduce_bias]),
        ((0, 10), (0, wide - share)),
    )
    attn_weights = jnp.concatenate([query_weight, key_weight, value_weight, out_weight.T], axis=1)
    attn_full, vectors_full, frames_all = transfers(
        1,
        "gather_first",
        [
            ("gather", ("clip",), attn_weights, BF16),
            ("gather", ("clip",), vectors, BF16),
            ("gather", ("ctx",), frames, BF16),
        ],
    )
    vectors_full = vectors_full.reshape(clips, 16, wide)[:, :6, :share]
    vectors_full = vectors_full.transpose(1, 0, 2).reshape(6, width).astype(F32)
    gain_first, shift_first, out_shift, gain_second, shift_second, reduce_shift = [
        vectors_full[i] for i in range(6)
    ]
    qkv_full = attn_full[:, : 3 * local_width]
    kv_full = attn_full[:, local_width : 3 * local_width]
    query_full = attn_full[:, :local_width]
    out_full_t = attn_full[:, 3 * local_width :]
    inputs = frames.astype(F32)
    normed_one, factor_one = center_rows(inputs)
    first_norm = (normed_one * gain_first + shift_first).astype(BF16)
    queries = (product(first_norm, query_full) + query_bias.astype(F32)).astype(BF16)
    normed_all, _ = center_rows(frames_all.astype(F32))
    norm_all = (normed_all * gain_first + shift_first).astype(BF16)
    kv_bias = jnp.concatenate([jnp.zeros_like(value_bias), value_bias]).astype(F32)
    kv_rows = (product(norm_all, kv_full) + kv_bias).astype(BF16)
    length = kv_rows.shape[0]
    query_heads = queries.reshape(row_count, head_count, DH)
    key_heads = kv_rows[:, :local_width].reshape(length, head_count, DH)
    value_heads = kv_rows[:, local_width:].reshape(length, head_count, DH)
    scores = (
        jnp.einsum("qhd,khd->qhk", query_heads, key_heads, preferred_element_type=F32)
        * score_scale
    )
    run_max = jnp.max(scores, axis=-1)
    weights = jnp.exp(scores - run_max[..., None])
    run_sum = jnp.sum(weights, axis=-1)
    run_acc = jnp.einsum(
        "qhk,khd->qhd", weights.astype(BF16), value_heads, preferred_element_type=F32
    )
    mixed_full = run_acc / run_sum[..., None]
    log_total = run_max + jnp.log(run_sum)
    mixed_low = mixed_full.reshape(row_count, local_width).astype(BF16)
    attn_sum, expand_full, reduce_full_t = transfers(
        2,
        "attn_sum",
        [
            ("reduce", ("tp",), cols_inner(mixed_low, out_full_t).astype(BF16), BF16),
            ("gather", ("clip",), expand_weight, BF16),
            ("gather", ("clip",), reduce_weight.T, BF16),
        ],
    )
    hidden = inputs + attn_sum.astype(F32) + out_shift
    normed_two, factor_two = center_rows(hidden)
    second_norm = (normed_two * gain_second + shift_second).astype(BF16)
    pre_act = product(second_norm, expand_full) + expand_bias.astype(F32)

    def gelu_exact(argument):
        return jax.nn.gelu(argument, approximate=False)

    activated, gelu_pull = jax.vjp(gelu_exact, pre_act)
    act_low = activated.astype(BF16)
    grad_act = product(cotangent, reduce_full_t)
    grad_pre = gelu_pull(grad_act)[0].astype(BF16)
    second_terms = cols_inner(grad_pre, expand_full).astype(BF16)
    grad_expand = rows_inner(second_norm, grad_pre).astype(BF16)
    grad_reduce_t = rows_inner(cotangent, act_low).astype(BF16)
    grad_second, share_expand, share_reduce_t = transfers(
        3,
        "grad_second",
        [
            ("reduce", ("tp",), second_terms, BF16),
            ("scatter", ("clip",), grad_expand, BF16),
            ("scatter", ("clip",), grad_reduce_t, BF16),
        ],
    )
    act_late, grad_second = lax.optimization_barrier((act_low, grad_second))
    mlp_sum = lax.psum(cols_inner(act_late, reduce_full_t).astype(BF16), "tp").astype(F32)
    layer_out = (hidden + mlp_sum + reduce_shift).astype(BF16)
    grad_out = cotangent.astype(F32)
    grad_second = grad_second.astype(F32)
    grad_hidden = grad_out + norm_back(grad_second, normed_two, factor_two, gain_second)
    grad_attn = grad_hidden.astype(BF16)
    grad_out_weight_t = rows_inner(grad_attn, mixed_low).astype(BF16)
    grad_mixed = product(grad_attn, out_full_t).astype(BF16)
    grad_heads = grad_mixed.reshape(row_count, head_count, DH)
    row_delta = jnp.sum(grad_heads.astype(F32) * mixed_full, axis=-1)
    weights_low, grad_scores = score_block(
        query_heads, key_heads, value_heads, grad_heads, log_total, row_delta, score_scale
    )
    grad_query = jnp.einsum("qhk,khd->qhd", grad_scores, key_heads, preferred_element_type=F32)
    key_term = jnp.einsum("qhk,qhd->khd", grad_scores, query_heads, preferred_element_type=F32)
    value_term = jnp.einsum("qhk,qhd->khd", weights_low, grad_heads, preferred_element_type=F32)
    kv_terms = jnp.concatenate(
        [
            (key_term * score_scale).reshape(length, local_width),
            value_term.reshape(length, local_width),
        ],
        axis=1,
    ).astype(BF16)
    (grad_kv_low,) = transfers(4, "grad_kv", [("scatter", ("ctx",), kv_terms, BF16)])
    grad_q_low = (grad_query * score_scale).reshape(row_count, local_width).astype(BF16)
    grad_qkv = jnp.concatenate([grad_q_low, grad_kv_low], axis=1)
    first_terms = cols_inner(grad_qkv, qkv_full).astype(BF16)
    grad_attn_weights = jnp.concatenate(
        [rows_inner(first_norm, grad_qkv).astype(BF16), grad_out_weight_t], axis=1
    )
    qkv_bias = jnp.sum(grad_qkv.astype(F32), axis=0)
    early = [
        jnp.sum(grad_out, axis=0),
        jnp.sum(grad_second * normed_two, axis=0),
        jnp.sum(grad_second, axis=0),
        jnp.sum(grad_attn.astype(F32), axis=0),
        jnp.sum(grad_pre.astype(F32), axis=0),
        qkv_bias[:local_width],
        qkv_bias[2 * local_width :],
    ]
    grad_first, sum_attn, sum_expand, sum_reduce_t, early_sum = transfers(
        5,
        "grad_first",
        [
            ("reduce", ("tp",), first_terms, BF16),
            ("both", ("clip",), grad_attn_weights, F32, ("ctx",)),
            ("share", ("ctx",), share_expand, F32),
            ("share", ("ctx",), share_reduce_t, F32),
            ("share", ("clip", "ctx"), pack_vectors(early), F32),
        ],
    )
    grad_first = grad_first.astype(F32)
    late = [jnp.sum(grad_first * normed_one, axis=0), jnp.sum(grad_first, axis=0)]
    (late_sum,) = transfers(
        6, "gain_sums", [("share", ("clip", "ctx"), pack_vectors(late), F32)]
    )
    frames_grad = grad_hidden + norm_back(grad_first, normed_one, factor_one, gain_first)

    def mine(vector):
        return lax.dynamic_slice(vector, (clip_at,), (share,))

    sums = unpack_vectors(
        early_sum, [width] * 4 + [hidden_width, local_width, local_width]
    )
    gain_one, shift_one = unpack_vectors(late_sum, [width] * 2)
    return (
        layer_out,
        frames_grad,
        mine(gain_one),
        mine(shift_one),
        sum_attn[:, :local_width],
        sums[5],
        sum_attn[:, local_width : 2 * local_width],
        sum_attn[:, 2 * local_width : 3 * local_width],
        sums[6],
        sum_attn[:, 3 * local_width :].T,
        mine(sums[3]),
        mine(sums[1]),
        mine(sums[2]),
        sum_expand,
        sums[4],
        sum_reduce_t.T,
        mine(sums[0]),
    )


def solution(mesh):
    placed = (
        P(("clip", "ctx"), None),
        P(("clip", "ctx"), None),
        P("clip"),
        P("clip"),
        P("clip", "tp"),
        P("tp"),
        P("clip", "tp"),
        P("clip", "tp"),
        P("tp"),
        P("tp", "clip"),
        P("clip"),
        P("clip"),
        P("clip"),
        P("clip", "tp"),
        P("tp"),
        P("tp", "clip"),
        P("clip"),
    )
    return jax.shard_map(
        shards,
        mesh=mesh,
        in_specs=placed,
        out_specs=(
            P(("clip", "ctx"), None),
            P(("clip", "ctx"), None),
            P("clip"),
            P("clip"),
            P("clip", "tp"),
            P("tp"),
            P("clip", "tp"),
            P("clip", "tp"),
            P("tp"),
            P("tp", "clip"),
            P("clip"),
            P("clip"),
            P("clip"),
            P("clip", "tp"),
            P("tp"),
            P("tp", "clip"),
            P("clip"),
        ),
        check_vma=False,
    )
```

```python
import functools
import itertools

import jax
import jax.numpy as jnp
from jax import lax
from jax.experimental import pallas as pl
from jax.experimental.pallas import tpu as pltpu
from jax.sharding import PartitionSpec as P

DH = 64


def center_rows(matrix):
    row_mean = jnp.mean(matrix, axis=-1, keepdims=True)
    centred = matrix - row_mean
    factor = lax.rsqrt(jnp.mean(centred * centred, axis=-1, keepdims=True) + 1e-05)
    return (centred * factor, factor)


def norm_back(grad_norm, normed, factor, gain):
    grad_hat = grad_norm * gain
    inner = jnp.mean(grad_hat, axis=-1, keepdims=True)
    cross = jnp.mean(grad_hat * normed, axis=-1, keepdims=True)
    return factor * (grad_hat - inner - normed * cross)


def product(left, right):
    return jnp.dot(left, right, preferred_element_type=jnp.float32)


def rows_inner(left, right):
    return lax.dot_general(
        left, right, (((0,), (0,)), ((), ())), preferred_element_type=jnp.float32
    )


def cols_inner(left, right):
    return lax.dot_general(
        left, right, (((1,), (1,)), ((), ())), preferred_element_type=jnp.float32
    )


def score_block(query_heads, key_heads, value_heads, grad_heads, log_total, row_delta, score_scale):
    scores = (
        jnp.einsum("qhd,khd->qhk", query_heads, key_heads, preferred_element_type=jnp.float32)
        * score_scale
    )
    weights = jnp.exp(scores - log_total[..., None])
    grad_weights = jnp.einsum(
        "qhd,khd->qhk", grad_heads, value_heads, preferred_element_type=jnp.float32
    )
    grad_scores = (weights * (grad_weights - row_delta[..., None])).astype(jnp.bfloat16)
    return (weights.astype(jnp.bfloat16), grad_scores)


F32 = jnp.float32
BF16 = jnp.bfloat16


def offsets(sizes):
    return [o for o in itertools.product(*(range(s) for s in sizes)) if any(o)]


def group_place(axes, sizes, offset):
    index = 0
    place = {}
    for axis, size, step in zip(axes, sizes, offset):
        at = lax.rem(lax.axis_index(axis) + step, size)
        place[axis] = at
        index = index * size + at
    return place, index


def rows_at(index, rows):
    return pl.ds(pl.multiple_of(index * rows, rows), rows)


def send(src, dst, sems, slot, place):
    copy = pltpu.make_async_remote_copy(
        src_ref=src,
        dst_ref=dst,
        send_sem=sems.at[0, slot],
        recv_sem=sems.at[1, slot],
        device_id=place,
        device_id_type=pl.DeviceIdType.MESH,
    )
    copy.start()
    return copy


def finish(copies):
    for copy in copies:
        copy.wait_send()


def spread(src, dst, rows, axes, sizes, sems):
    _, mine = group_place(axes, sizes, (0,) * len(axes))
    copies = []
    for slot, offset in enumerate(offsets(sizes)):
        place, _ = group_place(axes, sizes, offset)
        copies.append(send(src, dst.at[rows_at(mine, rows)], sems, slot, place))
    return mine, copies


def deal(src, landing, rows, axes, sizes, sems):
    copies = []
    for slot, offset in enumerate(offsets(sizes)):
        place, theirs = group_place(axes, sizes, offset)
        copies.append(send(src.at[rows_at(theirs, rows)], landing.at[slot], sems, slot, place))
    _, mine = group_place(axes, sizes, (0,) * len(axes))
    return mine, copies


def pair_places(axis):
    me = lax.axis_index(axis)
    near = me + 1 - 2 * lax.rem(me, 2)
    return me, near, lax.rem(me + 2, 4), lax.rem(near + 2, 4)


def gather_steps(axes, sizes, src, out, sems):
    rows = src.shape[0]
    if sizes == (4,) and axes == ("clip",):
        (axis,) = axes
        me, near, far, _ = pair_places(axis)
        mine = out.at[rows_at(me, rows)]
        theirs = out.at[rows_at(far, rows)]
        first = send(src, mine, sems, 0, {axis: far})
        second = send(src, mine, sems, 1, {axis: near})
        out[rows_at(me, rows), :] = src[...]
        yield
        first.wait_recv()
        third = send(theirs, theirs, sems, 2, {axis: near})
        yield
        second.wait_recv()
        third.wait_recv()
        finish([first, second, third])
    else:
        mine, copies = spread(src, out, rows, axes, sizes, sems)
        out[rows_at(mine, rows), :] = src[...]
        yield
        for copy in copies:
            copy.wait_recv()
        finish(copies)


def chain_steps(axes, sizes, more_axes, more_sizes, src, out, held, sems, more_sems):
    yield from gather_steps(axes, sizes, src, held, sems)
    yield from gather_steps(more_axes, more_sizes, held, out, more_sems)


def scatter_steps(axes, sizes, src, out, landing, part, sems):
    rows = out.shape[0]
    if sizes == (4,) and axes == ("clip",):
        (axis,) = axes
        me, near, far, near_far = pair_places(axis)
        copies = [
            send(src.at[rows_at(near_far, rows)], landing.at[1], sems, 1, {axis: near}),
            send(src.at[rows_at(near, rows)], landing.at[0], sems, 0, {axis: near}),
        ]
        yield
        copies[0].wait_recv()
        part[...] = (
            src[rows_at(far, rows), :].astype(F32) + landing[1].astype(F32)
        ).astype(part.dtype)
        copies.append(send(part, landing.at[2], sems, 2, {axis: far}))
        yield
        copies[1].wait_recv()
        copies[2].wait_recv()
        total = src[rows_at(me, rows), :].astype(F32) + landing[0].astype(F32)
        out[...] = (total + landing[2].astype(F32)).astype(out.dtype)
        finish(copies)
    else:
        mine, copies = deal(src, landing, rows, axes, sizes, sems)
        yield
        total = src[rows_at(mine, rows), :].astype(F32)
        for slot, copy in enumerate(copies):
            copy.wait_recv()
            total = total + landing[slot].astype(F32)
        out[...] = total.astype(out.dtype)
        finish(copies)


def reduce_steps(axes, sizes, src, out, landing, sems, back_sems):
    rows = landing.shape[1]
    mine, copies = deal(src, landing, rows, axes, sizes, sems)
    yield
    total = src[rows_at(mine, rows), :].astype(F32)
    for slot, copy in enumerate(copies):
        copy.wait_recv()
        total = total + landing[slot].astype(F32)
    block = rows_at(mine, rows)
    out[block, :] = total.astype(out.dtype)
    _, backs = spread(out.at[block], out, rows, axes, sizes, back_sems)
    yield
    for copy in backs:
        copy.wait_recv()
    finish(copies)
    finish(backs)


def sum_blocks(held, rows, count):
    total = held[0:rows, :].astype(F32)
    for index in range(1, count):
        total = total + held[index * rows : (index + 1) * rows, :].astype(F32)
    return total


def share_steps(axes, sizes, src, out, held, sems):
    rows = src.shape[0]
    mine, copies = spread(src, held, rows, axes, sizes, sems)
    held[rows_at(mine, rows), :] = src[...]
    yield
    for copy in copies:
        copy.wait_recv()
    out[...] = sum_blocks(held, rows, len(copies) + 1).astype(out.dtype)
    finish(copies)


def both_steps(
    axes, sizes, more_axes, more_sizes, src, out, landing, part, owned, held, sems, more_sems
):
    yield from scatter_steps(axes, sizes, src, owned, landing, part, sems)
    yield from share_steps(more_axes, more_sizes, owned, out, held, more_sems)


def plan_of(kind, axes, sizes, more, array, out_type):
    rows, cols = array.shape
    count = 1
    for size in sizes:
        count *= size
    peers = count - 1
    pair = pltpu.SemaphoreType.DMA((2, peers))
    if kind == "gather":
        return (count * rows, cols), [pair], functools.partial(gather_steps, axes, sizes)
    if kind == "share":
        held = pltpu.VMEM((count * rows, cols), array.dtype)
        return (rows, cols), [held, pair], functools.partial(share_steps, axes, sizes)
    if kind == "chain":
        more_axes, more_sizes = more
        more_count = 1
        for size in more_sizes:
            more_count *= size
        return (
            (more_count * count * rows, cols),
            [
                pltpu.VMEM((count * rows, cols), array.dtype),
                pair,
                pltpu.SemaphoreType.DMA((2, more_count - 1)),
            ],
            functools.partial(chain_steps, axes, sizes, more_axes, more_sizes),
        )
    block = rows // count
    one = pltpu.VMEM((block, cols), array.dtype)
    landing = pltpu.VMEM((peers, block, cols), array.dtype)
    if kind == "scatter":
        return (block, cols), [landing, one, pair], functools.partial(scatter_steps, axes, sizes)
    if kind == "reduce":
        return (
            (rows, cols),
            [landing, pair, pair],
            functools.partial(reduce_steps, axes, sizes),
        )
    more_axes, more_sizes = more
    more_count = 1
    for size in more_sizes:
        more_count *= size
    return (
        (block, cols),
        [
            landing,
            one,
            one,
            pltpu.VMEM((more_count * block, cols), array.dtype),
            pair,
            pltpu.SemaphoreType.DMA((2, more_count - 1)),
        ],
        functools.partial(both_steps, axes, sizes, more_axes, more_sizes),
    )


def transfers(collective_id, name, jobs):
    def sized(axes):
        return tuple(lax.axis_size(axis) for axis in axes)

    plans = []
    groups = []
    for job in jobs:
        kind, axes, array, out_type = job[:4]
        more = (job[4], sized(job[4])) if len(job) > 4 else None
        plans.append(plan_of(kind, axes, sized(axes), more, array, out_type))
        for group in (axes,) + ((job[4],) if len(job) > 4 else ()):
            if group not in groups:
                groups.append(group)
    places = {}
    for group in groups:
        for offset in offsets(sized(group)):
            key = tuple(sorted((a, o) for a, o in zip(group, offset) if o))
            places.setdefault(key, (group, offset))
    count = len(jobs)

    def kernel(*refs):
        sources, outs = refs[:count], refs[count : 2 * count]
        scratch = list(refs[2 * count :])
        barrier = pltpu.get_barrier_semaphore()
        for group, offset in places.values():
            place, _ = group_place(group, sized(group), offset)
            pl.semaphore_signal(
                barrier, inc=1, device_id=place, device_id_type=pl.DeviceIdType.MESH
            )
        pl.semaphore_wait(barrier, len(places))
        running = []
        for source, out, (_, needs, steps) in zip(sources, outs, plans):
            mine, scratch = scratch[: len(needs)], scratch[len(needs) :]
            running.append(steps(source, out, *mine))
        while running:
            running = [step for step in running if next(step, "end") != "end"]

    whole = pl.BlockSpec(memory_space=pltpu.VMEM)
    return pl.pallas_call(
        kernel,
        name=name,
        out_shape=[
            jax.ShapeDtypeStruct(plan[0], job[3]) for plan, job in zip(plans, jobs)
        ],
        in_specs=[whole] * count,
        out_specs=[whole] * count,
        scratch_shapes=[need for plan in plans for need in plan[1]],
        compiler_params=pltpu.CompilerParams(
            collective_id=collective_id,
            has_side_effects=True,
            vmem_limit_bytes=56 * 1024 * 1024,
        ),
    )(*[job[2] for job in jobs])


def pack_vectors(vectors):
    flat = jnp.concatenate(vectors)
    width = -(-flat.shape[0] // (8 * 128)) * 128
    return jnp.pad(flat, (0, 8 * width - flat.shape[0])).reshape(8, width)


def unpack_vectors(packed, sizes):
    flat = packed.reshape(-1)
    out = []
    at = 0
    for size in sizes:
        out.append(flat[at : at + size])
        at += size
    return out


def shards(
    frames,
    cotangent,
    first_gain,
    first_shift,
    query_weight,
    query_bias,
    key_weight,
    value_weight,
    value_bias,
    out_weight,
    out_bias,
    second_gain,
    second_shift,
    expand_weight,
    expand_bias,
    reduce_weight,
    reduce_bias,
):
    row_count, width = frames.shape
    local_width = query_weight.shape[1]
    head_count = local_width // DH
    score_scale = DH ** (-0.5)
    share = first_gain.shape[0]
    hidden_width = expand_weight.shape[1]
    clips = lax.axis_size("clip")
    clip_at = lax.axis_index("clip") * share
    wide = -(-share // 128) * 128
    vectors = jnp.pad(
        jnp.stack([first_gain, first_shift, out_bias, second_gain, second_shift, reduce_bias]),
        ((0, 10), (0, wide - share)),
    )
    attn_weights = jnp.concatenate([query_weight, key_weight, value_weight], axis=1)
    qkv_full, vectors_full, out_blocks, frames_all = transfers(
        1,
        "gather_first",
        [
            ("gather", ("clip",), attn_weights, BF16),
            ("gather", ("clip",), vectors, BF16),
            ("chain", ("tp",), out_weight, BF16, ("clip",)),
            ("gather", ("ctx",), frames, BF16),
        ],
    )
    vectors_full = vectors_full.reshape(clips, 16, wide)[:, :6, :share]
    vectors_full = vectors_full.transpose(1, 0, 2).reshape(6, width).astype(F32)
    gain_first, shift_first, out_shift, gain_second, shift_second, reduce_shift = [
        vectors_full[i] for i in range(6)
    ]
    kv_full = qkv_full[:, local_width:]
    query_full = qkv_full[:, :local_width]
    out_blocks = out_blocks.reshape(clips, width, share)
    out_all = out_blocks.transpose(1, 0, 2).reshape(width, width)
    out_rows = lax.dynamic_slice_in_dim(out_all, lax.axis_index("tp") * local_width, local_width)
    inputs = frames.astype(F32)
    normed_one, factor_one = center_rows(inputs)
    first_norm = (normed_one * gain_first + shift_first).astype(BF16)
    queries = (product(first_norm, query_full) + query_bias.astype(F32)).astype(BF16)
    normed_all, _ = center_rows(frames_all.astype(F32))
    norm_all = (normed_all * gain_first + shift_first).astype(BF16)
    kv_bias = jnp.concatenate([jnp.zeros_like(value_bias), value_bias]).astype(F32)
    kv_rows = (product(norm_all, kv_full) + kv_bias).astype(BF16)
    length = kv_rows.shape[0]
    query_heads = queries.reshape(row_count, head_count, DH)
    key_heads = kv_rows[:, :local_width].reshape(length, head_count, DH)
    value_heads = kv_rows[:, local_width:].reshape(length, head_count, DH)
    scores = (
        jnp.einsum("qhd,khd->qhk", query_heads, key_heads, preferred_element_type=F32)
        * score_scale
    )
    run_max = jnp.max(scores, axis=-1)
    weights = jnp.exp(scores - run_max[..., None])
    run_sum = jnp.sum(weights, axis=-1)
    run_acc = jnp.einsum(
        "qhk,khd->qhd", weights.astype(BF16), value_heads, preferred_element_type=F32
    )
    mixed_full = run_acc / run_sum[..., None]
    log_total = run_max + jnp.log(run_sum)
    mixed_low = mixed_full.reshape(row_count, local_width).astype(BF16)
    expand_full, reduce_full_t, mixed_all = transfers(
        2,
        "gather_mixed",
        [
            ("gather", ("clip",), expand_weight, BF16),
            ("gather", ("clip",), reduce_weight.T, BF16),
            ("gather", ("tp",), mixed_low, BF16),
        ],
    )
    groups = width // local_width
    mixed_all = mixed_all.reshape(groups, row_count, local_width)
    mixed_all = mixed_all.transpose(1, 0, 2).reshape(row_count, width)
    hidden = inputs + product(mixed_all, out_all) + out_shift
    normed_two, factor_two = center_rows(hidden)
    second_norm = (normed_two * gain_second + shift_second).astype(BF16)
    pre_act = product(second_norm, expand_full) + expand_bias.astype(F32)

    def gelu_exact(argument):
        return jax.nn.gelu(argument, approximate=False)

    activated, gelu_pull = jax.vjp(gelu_exact, pre_act)
    act_low = activated.astype(BF16)
    grad_act = product(cotangent, reduce_full_t)
    grad_pre = gelu_pull(grad_act)[0].astype(BF16)
    second_terms = cols_inner(grad_pre, expand_full).astype(BF16)
    grad_expand = rows_inner(second_norm, grad_pre).astype(BF16)
    grad_reduce_t = rows_inner(cotangent, act_low).astype(BF16)
    share_expand, share_reduce_t, grad_second = transfers(
        3,
        "grad_second",
        [
            ("scatter", ("clip",), grad_expand, BF16),
            ("scatter", ("clip",), grad_reduce_t, BF16),
            ("reduce", ("tp",), second_terms, BF16),
        ],
    )
    mlp_terms = cols_inner(act_low, reduce_full_t).astype(BF16)
    grad_out = cotangent.astype(F32)
    grad_second = grad_second.astype(F32)
    grad_hidden = grad_out + norm_back(grad_second, normed_two, factor_two, gain_second)
    grad_attn = grad_hidden.astype(BF16)
    grad_out_weight_t = rows_inner(grad_attn, mixed_low).astype(BF16)
    grad_mixed = cols_inner(grad_attn, out_rows).astype(BF16)
    grad_heads = grad_mixed.reshape(row_count, head_count, DH)
    row_delta = jnp.sum(grad_heads.astype(F32) * mixed_full, axis=-1)
    weights_low, grad_scores = score_block(
        query_heads, key_heads, value_heads, grad_heads, log_total, row_delta, score_scale
    )
    grad_query = jnp.einsum("qhk,khd->qhd", grad_scores, key_heads, preferred_element_type=F32)
    key_term = jnp.einsum("qhk,qhd->khd", grad_scores, query_heads, preferred_element_type=F32)
    value_term = jnp.einsum("qhk,qhd->khd", weights_low, grad_heads, preferred_element_type=F32)
    kv_terms = jnp.concatenate(
        [
            (key_term * score_scale).reshape(length, local_width),
            value_term.reshape(length, local_width),
        ],
        axis=1,
    ).astype(BF16)
    grad_kv_low, mlp_sum = transfers(
        4,
        "grad_kv",
        [("scatter", ("ctx",), kv_terms, BF16), ("reduce", ("tp",), mlp_terms, BF16)],
    )
    layer_out = (hidden + mlp_sum.astype(F32) + reduce_shift).astype(BF16)
    grad_q_low = (grad_query * score_scale).reshape(row_count, local_width).astype(BF16)
    grad_qkv = jnp.concatenate([grad_q_low, grad_kv_low], axis=1)
    first_terms = cols_inner(grad_qkv, qkv_full).astype(BF16)
    grad_attn_weights = jnp.concatenate(
        [rows_inner(first_norm, grad_qkv).astype(BF16), grad_out_weight_t], axis=1
    )
    qkv_bias = jnp.sum(grad_qkv.astype(F32), axis=0)
    early = [
        jnp.sum(grad_out, axis=0),
        jnp.sum(grad_second * normed_two, axis=0),
        jnp.sum(grad_second, axis=0),
        jnp.sum(grad_attn.astype(F32), axis=0),
        jnp.sum(grad_pre.astype(F32), axis=0),
        qkv_bias[:local_width],
        qkv_bias[2 * local_width :],
    ]
    sum_attn, grad_first, sum_expand, sum_reduce_t, early_sum = transfers(
        5,
        "grad_first",
        [
            ("both", ("clip",), grad_attn_weights, F32, ("ctx",)),
            ("reduce", ("tp",), first_terms, BF16),
            ("share", ("ctx",), share_expand, F32),
            ("share", ("ctx",), share_reduce_t, F32),
            ("share", ("clip", "ctx"), pack_vectors(early), F32),
        ],
    )
    grad_first = grad_first.astype(F32)
    late = [jnp.sum(grad_first * normed_one, axis=0), jnp.sum(grad_first, axis=0)]
    (late_sum,) = transfers(
        6, "gain_sums", [("share", ("clip", "ctx"), pack_vectors(late), F32)]
    )
    frames_grad = grad_hidden + norm_back(grad_first, normed_one, factor_one, gain_first)

    def mine(vector):
        return lax.dynamic_slice(vector, (clip_at,), (share,))

    sums = unpack_vectors(
        early_sum, [width] * 4 + [hidden_width, local_width, local_width]
    )
    gain_one, shift_one = unpack_vectors(late_sum, [width] * 2)
    return (
        layer_out,
        frames_grad,
        mine(gain_one),
        mine(shift_one),
        sum_attn[:, :local_width],
        sums[5],
        sum_attn[:, local_width : 2 * local_width],
        sum_attn[:, 2 * local_width : 3 * local_width],
        sums[6],
        sum_attn[:, 3 * local_width :].T,
        mine(sums[3]),
        mine(sums[1]),
        mine(sums[2]),
        sum_expand,
        sums[4],
        sum_reduce_t.T,
        mine(sums[0]),
    )


def solution(mesh):
    placed = (
        P(("clip", "ctx"), None),
        P(("clip", "ctx"), None),
        P("clip"),
        P("clip"),
        P("clip", "tp"),
        P("tp"),
        P("clip", "tp"),
        P("clip", "tp"),
        P("tp"),
        P("tp", "clip"),
        P("clip"),
        P("clip"),
        P("clip"),
        P("clip", "tp"),
        P("tp"),
        P("tp", "clip"),
        P("clip"),
    )
    return jax.shard_map(
        shards,
        mesh=mesh,
        in_specs=placed,
        out_specs=(
            P(("clip", "ctx"), None),
            P(("clip", "ctx"), None),
            P("clip"),
            P("clip"),
            P("clip", "tp"),
            P("tp"),
            P("clip", "tp"),
            P("clip", "tp"),
            P("tp"),
            P("tp", "clip"),
            P("clip"),
            P("clip"),
            P("clip"),
            P("clip", "tp"),
            P("tp"),
            P("tp", "clip"),
            P("clip"),
        ),
        check_vma=False,
    )
```

```python
import functools
import itertools

import jax
import jax.numpy as jnp
from jax import lax
from jax.experimental import pallas as pl
from jax.experimental.pallas import tpu as pltpu
from jax.sharding import PartitionSpec as P

DH = 64


def center_rows(matrix):
    row_mean = jnp.mean(matrix, axis=-1, keepdims=True)
    centred = matrix - row_mean
    factor = lax.rsqrt(jnp.mean(centred * centred, axis=-1, keepdims=True) + 1e-05)
    return (centred * factor, factor)


def norm_back(grad_norm, normed, factor, gain):
    grad_hat = grad_norm * gain
    inner = jnp.mean(grad_hat, axis=-1, keepdims=True)
    cross = jnp.mean(grad_hat * normed, axis=-1, keepdims=True)
    return factor * (grad_hat - inner - normed * cross)


def product(left, right):
    return jnp.dot(left, right, preferred_element_type=jnp.float32)


def rows_inner(left, right):
    return lax.dot_general(
        left, right, (((0,), (0,)), ((), ())), preferred_element_type=jnp.float32
    )


def cols_inner(left, right):
    return lax.dot_general(
        left, right, (((1,), (1,)), ((), ())), preferred_element_type=jnp.float32
    )


def score_block(query_heads, key_heads, value_heads, grad_heads, log_total, row_delta, score_scale):
    scores = (
        jnp.einsum("qhd,khd->qhk", query_heads, key_heads, preferred_element_type=jnp.float32)
        * score_scale
    )
    weights = jnp.exp(scores - log_total[..., None])
    grad_weights = jnp.einsum(
        "qhd,khd->qhk", grad_heads, value_heads, preferred_element_type=jnp.float32
    )
    grad_scores = (weights * (grad_weights - row_delta[..., None])).astype(jnp.bfloat16)
    return (weights.astype(jnp.bfloat16), grad_scores)


F32 = jnp.float32
BF16 = jnp.bfloat16


def offsets(sizes):
    return [o for o in itertools.product(*(range(s) for s in sizes)) if any(o)]


def group_place(axes, sizes, offset):
    index = 0
    place = {}
    for axis, size, step in zip(axes, sizes, offset):
        at = lax.rem(lax.axis_index(axis) + step, size)
        place[axis] = at
        index = index * size + at
    return place, index


def rows_at(index, rows):
    return pl.ds(pl.multiple_of(index * rows, rows), rows)


def send(src, dst, sems, slot, place):
    copy = pltpu.make_async_remote_copy(
        src_ref=src,
        dst_ref=dst,
        send_sem=sems.at[0, slot],
        recv_sem=sems.at[1, slot],
        device_id=place,
        device_id_type=pl.DeviceIdType.MESH,
    )
    copy.start()
    return copy


def finish(copies):
    for copy in copies:
        copy.wait_send()


def spread(src, dst, rows, axes, sizes, sems):
    _, mine = group_place(axes, sizes, (0,) * len(axes))
    copies = []
    for slot, offset in enumerate(offsets(sizes)):
        place, _ = group_place(axes, sizes, offset)
        copies.append(send(src, dst.at[rows_at(mine, rows)], sems, slot, place))
    return mine, copies


def deal(src, landing, rows, axes, sizes, sems):
    copies = []
    for slot, offset in enumerate(offsets(sizes)):
        place, theirs = group_place(axes, sizes, offset)
        copies.append(send(src.at[rows_at(theirs, rows)], landing.at[slot], sems, slot, place))
    _, mine = group_place(axes, sizes, (0,) * len(axes))
    return mine, copies


def pair_places(axis):
    me = lax.axis_index(axis)
    near = me + 1 - 2 * lax.rem(me, 2)
    return me, near, lax.rem(me + 2, 4), lax.rem(near + 2, 4)


def gather_steps(axes, sizes, src, out, sems):
    rows = src.shape[0]
    if sizes == (4,) and axes == ("clip",):
        (axis,) = axes
        me, near, far, _ = pair_places(axis)
        mine = out.at[rows_at(me, rows)]
        theirs = out.at[rows_at(far, rows)]
        first = send(src, mine, sems, 0, {axis: far})
        second = send(src, mine, sems, 1, {axis: near})
        out[rows_at(me, rows), :] = src[...]
        yield
        first.wait_recv()
        third = send(theirs, theirs, sems, 2, {axis: near})
        yield
        second.wait_recv()
        third.wait_recv()
        finish([first, second, third])
    else:
        mine, copies = spread(src, out, rows, axes, sizes, sems)
        out[rows_at(mine, rows), :] = src[...]
        yield
        for copy in copies:
            copy.wait_recv()
        finish(copies)


def chain_steps(axes, sizes, more_axes, more_sizes, src, out, held, sems, more_sems):
    yield from gather_steps(axes, sizes, src, held, sems)
    yield from gather_steps(more_axes, more_sizes, held, out, more_sems)


def scatter_steps(axes, sizes, src, out, landing, part, sems):
    rows = out.shape[0]
    if sizes == (4,) and axes == ("clip",):
        (axis,) = axes
        me, near, far, near_far = pair_places(axis)
        copies = [
            send(src.at[rows_at(near_far, rows)], landing.at[1], sems, 1, {axis: near}),
            send(src.at[rows_at(near, rows)], landing.at[0], sems, 0, {axis: near}),
        ]
        yield
        copies[0].wait_recv()
        part[...] = (
            src[rows_at(far, rows), :].astype(F32) + landing[1].astype(F32)
        ).astype(part.dtype)
        copies.append(send(part, landing.at[2], sems, 2, {axis: far}))
        yield
        copies[1].wait_recv()
        copies[2].wait_recv()
        total = src[rows_at(me, rows), :].astype(F32) + landing[0].astype(F32)
        out[...] = (total + landing[2].astype(F32)).astype(out.dtype)
        finish(copies)
    else:
        mine, copies = deal(src, landing, rows, axes, sizes, sems)
        yield
        total = src[rows_at(mine, rows), :].astype(F32)
        for slot, copy in enumerate(copies):
            copy.wait_recv()
            total = total + landing[slot].astype(F32)
        out[...] = total.astype(out.dtype)
        finish(copies)


def reduce_steps(axes, sizes, src, out, landing, sems, back_sems):
    rows = landing.shape[1]
    mine, copies = deal(src, landing, rows, axes, sizes, sems)
    yield
    total = src[rows_at(mine, rows), :].astype(F32)
    for slot, copy in enumerate(copies):
        copy.wait_recv()
        total = total + landing[slot].astype(F32)
    block = rows_at(mine, rows)
    out[block, :] = total.astype(out.dtype)
    _, backs = spread(out.at[block], out, rows, axes, sizes, back_sems)
    yield
    for copy in backs:
        copy.wait_recv()
    finish(copies)
    finish(backs)


def sum_blocks(held, rows, count):
    total = held[0:rows, :].astype(F32)
    for index in range(1, count):
        total = total + held[index * rows : (index + 1) * rows, :].astype(F32)
    return total


def share_steps(axes, sizes, src, out, held, sems):
    rows = src.shape[0]
    mine, copies = spread(src, held, rows, axes, sizes, sems)
    held[rows_at(mine, rows), :] = src[...]
    yield
    for copy in copies:
        copy.wait_recv()
    out[...] = sum_blocks(held, rows, len(copies) + 1).astype(out.dtype)
    finish(copies)


def both_steps(
    axes, sizes, more_axes, more_sizes, src, out, landing, part, owned, held, sems, more_sems
):
    yield from scatter_steps(axes, sizes, src, owned, landing, part, sems)
    yield from share_steps(more_axes, more_sizes, owned, out, held, more_sems)


def plan_of(kind, axes, sizes, more, array, out_type):
    rows, cols = array.shape
    count = 1
    for size in sizes:
        count *= size
    peers = count - 1
    pair = pltpu.SemaphoreType.DMA((2, peers))
    if kind == "gather":
        return (count * rows, cols), [pair], functools.partial(gather_steps, axes, sizes)
    if kind == "share":
        held = pltpu.VMEM((count * rows, cols), array.dtype)
        return (rows, cols), [held, pair], functools.partial(share_steps, axes, sizes)
    if kind == "chain":
        more_axes, more_sizes = more
        more_count = 1
        for size in more_sizes:
            more_count *= size
        return (
            (more_count * count * rows, cols),
            [
                pltpu.VMEM((count * rows, cols), array.dtype),
                pair,
                pltpu.SemaphoreType.DMA((2, more_count - 1)),
            ],
            functools.partial(chain_steps, axes, sizes, more_axes, more_sizes),
        )
    block = rows // count
    one = pltpu.VMEM((block, cols), array.dtype)
    landing = pltpu.VMEM((peers, block, cols), array.dtype)
    if kind == "scatter":
        return (block, cols), [landing, one, pair], functools.partial(scatter_steps, axes, sizes)
    if kind == "reduce":
        return (
            (rows, cols),
            [landing, pair, pair],
            functools.partial(reduce_steps, axes, sizes),
        )
    more_axes, more_sizes = more
    more_count = 1
    for size in more_sizes:
        more_count *= size
    return (
        (block, cols),
        [
            landing,
            one,
            one,
            pltpu.VMEM((more_count * block, cols), array.dtype),
            pair,
            pltpu.SemaphoreType.DMA((2, more_count - 1)),
        ],
        functools.partial(both_steps, axes, sizes, more_axes, more_sizes),
    )


def transfers(collective_id, name, jobs):
    def sized(axes):
        return tuple(lax.axis_size(axis) for axis in axes)

    plans = []
    groups = []
    for job in jobs:
        kind, axes, array, out_type = job[:4]
        more = (job[4], sized(job[4])) if len(job) > 4 else None
        plans.append(plan_of(kind, axes, sized(axes), more, array, out_type))
        for group in (axes,) + ((job[4],) if len(job) > 4 else ()):
            if group not in groups:
                groups.append(group)
    places = {}
    for group in groups:
        for offset in offsets(sized(group)):
            key = tuple(sorted((a, o) for a, o in zip(group, offset) if o))
            places.setdefault(key, (group, offset))
    count = len(jobs)

    def kernel(*refs):
        sources, outs = refs[:count], refs[count : 2 * count]
        scratch = list(refs[2 * count :])
        barrier = pltpu.get_barrier_semaphore()
        for group, offset in places.values():
            place, _ = group_place(group, sized(group), offset)
            pl.semaphore_signal(
                barrier, inc=1, device_id=place, device_id_type=pl.DeviceIdType.MESH
            )
        pl.semaphore_wait(barrier, len(places))
        running = []
        for source, out, (_, needs, steps) in zip(sources, outs, plans):
            mine, scratch = scratch[: len(needs)], scratch[len(needs) :]
            running.append(steps(source, out, *mine))
        while running:
            running = [step for step in running if next(step, "end") != "end"]

    whole = pl.BlockSpec(memory_space=pltpu.VMEM)
    return pl.pallas_call(
        kernel,
        name=name,
        out_shape=[
            jax.ShapeDtypeStruct(plan[0], job[3]) for plan, job in zip(plans, jobs)
        ],
        in_specs=[whole] * count,
        out_specs=[whole] * count,
        scratch_shapes=[need for plan in plans for need in plan[1]],
        compiler_params=pltpu.CompilerParams(
            collective_id=collective_id,
            has_side_effects=True,
            vmem_limit_bytes=56 * 1024 * 1024,
        ),
    )(*[job[2] for job in jobs])


def pack_vectors(vectors):
    flat = jnp.concatenate(vectors)
    width = -(-flat.shape[0] // (8 * 128)) * 128
    return jnp.pad(flat, (0, 8 * width - flat.shape[0])).reshape(8, width)


def unpack_vectors(packed, sizes):
    flat = packed.reshape(-1)
    out = []
    at = 0
    for size in sizes:
        out.append(flat[at : at + size])
        at += size
    return out


def shards(
    frames,
    cotangent,
    first_gain,
    first_shift,
    query_weight,
    query_bias,
    key_weight,
    value_weight,
    value_bias,
    out_weight,
    out_bias,
    second_gain,
    second_shift,
    expand_weight,
    expand_bias,
    reduce_weight,
    reduce_bias,
):
    row_count, width = frames.shape
    local_width = query_weight.shape[1]
    head_count = local_width // DH
    score_scale = DH ** (-0.5)
    share = first_gain.shape[0]
    hidden_width = expand_weight.shape[1]
    clips = lax.axis_size("clip")
    clip_at = lax.axis_index("clip") * share
    flat = jnp.concatenate(
        [first_gain, first_shift, out_bias, second_gain, second_shift, reduce_bias]
    )
    wide = -(-flat.shape[0] // (16 * 128)) * 128
    vectors = jnp.pad(flat, (0, 16 * wide - flat.shape[0])).reshape(16, wide)
    half = local_width // 2
    out_packed = jnp.concatenate([out_weight[:half], out_weight[half:]], axis=1)
    attn_weights = jnp.concatenate([query_weight, key_weight, value_weight], axis=1)
    qkv_full, vectors_full, out_blocks, frames_all = transfers(
        1,
        "gather_first",
        [
            ("gather", ("clip",), attn_weights, BF16),
            ("gather", ("clip",), vectors, BF16),
            ("chain", ("tp",), out_packed, BF16, ("clip",)),
            ("gather", ("ctx",), frames, BF16),
        ],
    )
    vectors_full = vectors_full.reshape(clips, 16 * wide)[:, : 6 * share].reshape(clips, 6, share)
    vectors_full = vectors_full.transpose(1, 0, 2).reshape(6, width).astype(F32)
    gain_first, shift_first, out_shift, gain_second, shift_second, reduce_shift = [
        vectors_full[i] for i in range(6)
    ]
    kv_full = qkv_full[:, local_width:]
    query_full = qkv_full[:, :local_width]
    groups = width // local_width
    out_blocks = out_blocks.reshape(clips, groups, half, 2, share)
    out_all = out_blocks.transpose(1, 3, 2, 0, 4).reshape(width, width)
    out_rows = lax.dynamic_slice_in_dim(out_all, lax.axis_index("tp") * local_width, local_width)
    inputs = frames.astype(F32)
    normed_one, factor_one = center_rows(inputs)
    first_norm = (normed_one * gain_first + shift_first).astype(BF16)
    queries = (product(first_norm, query_full) + query_bias.astype(F32)).astype(BF16)
    normed_all, _ = center_rows(frames_all.astype(F32))
    norm_all = (normed_all * gain_first + shift_first).astype(BF16)
    kv_bias = jnp.concatenate([jnp.zeros_like(value_bias), value_bias]).astype(F32)
    kv_rows = (product(norm_all, kv_full) + kv_bias).astype(BF16)
    length = kv_rows.shape[0]
    query_heads = queries.reshape(row_count, head_count, DH)
    key_heads = kv_rows[:, :local_width].reshape(length, head_count, DH)
    value_heads = kv_rows[:, local_width:].reshape(length, head_count, DH)
    scores = (
        jnp.einsum("qhd,khd->qhk", query_heads, key_heads, preferred_element_type=F32)
        * score_scale
    )
    run_max = jnp.max(scores, axis=-1)
    weights = jnp.exp(scores - run_max[..., None])
    run_sum = jnp.sum(weights, axis=-1)
    run_acc = jnp.einsum(
        "qhk,khd->qhd", weights.astype(BF16), value_heads, preferred_element_type=F32
    )
    mixed_full = run_acc / run_sum[..., None]
    log_total = run_max + jnp.log(run_sum)
    mixed_low = mixed_full.reshape(row_count, local_width).astype(BF16)
    expand_full, reduce_full_t, mixed_all = transfers(
        2,
        "gather_mixed",
        [
            ("gather", ("clip",), expand_weight, BF16),
            ("gather", ("clip",), reduce_weight.T, BF16),
            ("gather", ("tp",), mixed_low.T, BF16),
        ],
    )
    hidden = inputs + rows_inner(mixed_all, out_all) + out_shift
    normed_two, factor_two = center_rows(hidden)
    second_norm = (normed_two * gain_second + shift_second).astype(BF16)
    pre_act = product(second_norm, expand_full) + expand_bias.astype(F32)

    def gelu_exact(argument):
        return jax.nn.gelu(argument, approximate=False)

    activated, gelu_pull = jax.vjp(gelu_exact, pre_act)
    act_low = activated.astype(BF16)
    grad_act = product(cotangent, reduce_full_t)
    grad_pre = gelu_pull(grad_act)[0].astype(BF16)
    second_terms = cols_inner(grad_pre, expand_full).astype(BF16)
    grad_expand = rows_inner(second_norm, grad_pre).astype(BF16)
    grad_reduce_t = rows_inner(cotangent, act_low).astype(BF16)
    share_expand, share_reduce_t, grad_second = transfers(
        3,
        "grad_second",
        [
            ("scatter", ("clip",), grad_expand, BF16),
            ("scatter", ("clip",), grad_reduce_t, BF16),
            ("reduce", ("tp",), second_terms, BF16),
        ],
    )
    act_late, grad_second = lax.optimization_barrier((act_low, grad_second))
    mlp_terms = cols_inner(act_late, reduce_full_t).astype(BF16)
    tp_size = lax.axis_size("tp")
    tp_at = lax.axis_index("tp")
    part_rows = row_count // tp_size

    def mlp_block(index):
        return lax.dynamic_slice_in_dim(mlp_terms, index * part_rows, part_rows)

    mlp_parts = [mlp_block(tp_at)]
    for step in range(1, tp_size):
        ring = [(i, (i + step) % tp_size) for i in range(tp_size)]
        mlp_parts.append(lax.ppermute(mlp_block((tp_at + step) % tp_size), "tp", ring))
    grad_out = cotangent.astype(F32)
    grad_second = grad_second.astype(F32)
    grad_hidden = grad_out + norm_back(grad_second, normed_two, factor_two, gain_second)
    grad_attn = grad_hidden.astype(BF16)
    grad_out_weight_t = rows_inner(grad_attn, mixed_low).astype(BF16)
    grad_mixed = cols_inner(grad_attn, out_rows).astype(BF16)
    grad_heads = grad_mixed.reshape(row_count, head_count, DH)
    row_delta = jnp.sum(grad_heads.astype(F32) * mixed_full, axis=-1)
    weights_low, grad_scores = score_block(
        query_heads, key_heads, value_heads, grad_heads, log_total, row_delta, score_scale
    )
    grad_query = jnp.einsum("qhk,khd->qhd", grad_scores, key_heads, preferred_element_type=F32)
    key_term = jnp.einsum("qhk,qhd->khd", grad_scores, query_heads, preferred_element_type=F32)
    value_term = jnp.einsum("qhk,qhd->khd", weights_low, grad_heads, preferred_element_type=F32)
    kv_terms = jnp.concatenate(
        [
            (key_term * score_scale).reshape(length, local_width),
            value_term.reshape(length, local_width),
        ],
        axis=1,
    ).astype(BF16)
    mlp_part = mlp_parts[0].astype(F32)
    for part in mlp_parts[1:]:
        mlp_part = mlp_part + part.astype(F32)
    grad_kv_low, mlp_sum = transfers(
        4,
        "grad_kv",
        [
            ("scatter", ("ctx",), kv_terms, BF16),
            ("gather", ("tp",), mlp_part.astype(BF16), BF16),
        ],
    )
    layer_out = (hidden + mlp_sum.astype(F32) + reduce_shift).astype(BF16)
    grad_q_low = (grad_query * score_scale).reshape(row_count, local_width).astype(BF16)
    grad_qkv = jnp.concatenate([grad_q_low, grad_kv_low], axis=1)
    first_terms = cols_inner(grad_qkv, qkv_full).astype(BF16)
    grad_attn_weights = jnp.concatenate(
        [rows_inner(first_norm, grad_qkv).astype(BF16), grad_out_weight_t], axis=1
    )
    qkv_bias = jnp.sum(grad_qkv.astype(F32), axis=0)
    early = [
        jnp.sum(grad_out, axis=0),
        jnp.sum(grad_second * normed_two, axis=0),
        jnp.sum(grad_second, axis=0),
        jnp.sum(grad_attn.astype(F32), axis=0),
        jnp.sum(grad_pre.astype(F32), axis=0),
        qkv_bias[:local_width],
        qkv_bias[2 * local_width :],
    ]
    sum_attn, grad_first, sum_expand, sum_reduce_t, early_sum = transfers(
        5,
        "grad_first",
        [
            ("both", ("clip",), grad_attn_weights, F32, ("ctx",)),
            ("reduce", ("tp",), first_terms, BF16),
            ("share", ("ctx",), share_expand, F32),
            ("share", ("ctx",), share_reduce_t, F32),
            ("share", ("clip", "ctx"), pack_vectors(early), F32),
        ],
    )
    grad_first = grad_first.astype(F32)
    late = [jnp.sum(grad_first * normed_one, axis=0), jnp.sum(grad_first, axis=0)]
    (late_sum,) = transfers(
        6, "gain_sums", [("share", ("clip", "ctx"), pack_vectors(late), F32)]
    )
    frames_grad = grad_hidden + norm_back(grad_first, normed_one, factor_one, gain_first)

    sums = unpack_vectors(early_sum, [4 * width, hidden_width, local_width, local_width])
    (late_sums,) = unpack_vectors(late_sum, [2 * width])
    shared = jnp.concatenate([sums[0], late_sums]).reshape(6, width)
    shared = lax.dynamic_slice(shared, (0, clip_at), (6, share))
    return (
        layer_out,
        frames_grad,
        shared[4],
        shared[5],
        sum_attn[:, :local_width],
        sums[2],
        sum_attn[:, local_width : 2 * local_width],
        sum_attn[:, 2 * local_width : 3 * local_width],
        sums[3],
        sum_attn[:, 3 * local_width :].T,
        shared[3],
        shared[1],
        shared[2],
        sum_expand,
        sums[1],
        sum_reduce_t.T,
        shared[0],
    )


def solution(mesh):
    placed = (
        P(("clip", "ctx"), None),
        P(("clip", "ctx"), None),
        P("clip"),
        P("clip"),
        P("clip", "tp"),
        P("tp"),
        P("clip", "tp"),
        P("clip", "tp"),
        P("tp"),
        P("tp", "clip"),
        P("clip"),
        P("clip"),
        P("clip"),
        P("clip", "tp"),
        P("tp"),
        P("tp", "clip"),
        P("clip"),
    )
    return jax.shard_map(
        shards,
        mesh=mesh,
        in_specs=placed,
        out_specs=(
            P(("clip", "ctx"), None),
            P(("clip", "ctx"), None),
            P("clip"),
            P("clip"),
            P("clip", "tp"),
            P("tp"),
            P("clip", "tp"),
            P("clip", "tp"),
            P("tp"),
            P("tp", "clip"),
            P("clip"),
            P("clip"),
            P("clip"),
            P("clip", "tp"),
            P("tp"),
            P("tp", "clip"),
            P("clip"),
        ),
        check_vma=False,
    )
```

```python
import functools
import itertools

import jax
import jax.numpy as jnp
from jax import lax
from jax.experimental import pallas as pl
from jax.experimental.pallas import tpu as pltpu
from jax.sharding import PartitionSpec as P

DH = 64


def center_rows(matrix):
    row_mean = jnp.mean(matrix, axis=-1, keepdims=True)
    centred = matrix - row_mean
    factor = lax.rsqrt(jnp.mean(centred * centred, axis=-1, keepdims=True) + 1e-05)
    return (centred * factor, factor)


def norm_back(grad_norm, normed, factor, gain):
    grad_hat = grad_norm * gain
    inner = jnp.mean(grad_hat, axis=-1, keepdims=True)
    cross = jnp.mean(grad_hat * normed, axis=-1, keepdims=True)
    return factor * (grad_hat - inner - normed * cross)


def product(left, right):
    return jnp.dot(left, right, preferred_element_type=jnp.float32)


def rows_inner(left, right):
    return lax.dot_general(
        left, right, (((0,), (0,)), ((), ())), preferred_element_type=jnp.float32
    )


def cols_inner(left, right):
    return lax.dot_general(
        left, right, (((1,), (1,)), ((), ())), preferred_element_type=jnp.float32
    )


def score_block(query_heads, key_heads, value_heads, grad_heads, log_total, row_delta, score_scale):
    scores = (
        jnp.einsum("qhd,khd->qhk", query_heads, key_heads, preferred_element_type=jnp.float32)
        * score_scale
    )
    weights = jnp.exp(scores - log_total[..., None])
    grad_weights = jnp.einsum(
        "qhd,khd->qhk", grad_heads, value_heads, preferred_element_type=jnp.float32
    )
    grad_scores = (weights * (grad_weights - row_delta[..., None])).astype(jnp.bfloat16)
    return (weights.astype(jnp.bfloat16), grad_scores)


F32 = jnp.float32
BF16 = jnp.bfloat16


def offsets(sizes):
    return [o for o in itertools.product(*(range(s) for s in sizes)) if any(o)]


def group_place(axes, sizes, offset):
    index = 0
    place = {}
    for axis, size, step in zip(axes, sizes, offset):
        at = lax.rem(lax.axis_index(axis) + step, size)
        place[axis] = at
        index = index * size + at
    return place, index


def rows_at(index, rows):
    return pl.ds(pl.multiple_of(index * rows, rows), rows)


def send(src, dst, sems, slot, place):
    copy = pltpu.make_async_remote_copy(
        src_ref=src,
        dst_ref=dst,
        send_sem=sems.at[0, slot],
        recv_sem=sems.at[1, slot],
        device_id=place,
        device_id_type=pl.DeviceIdType.MESH,
    )
    copy.start()
    return copy


def finish(copies):
    for copy in copies:
        copy.wait_send()


def spread(src, dst, rows, axes, sizes, sems):
    _, mine = group_place(axes, sizes, (0,) * len(axes))
    copies = []
    for slot, offset in enumerate(offsets(sizes)):
        place, _ = group_place(axes, sizes, offset)
        copies.append(send(src, dst.at[rows_at(mine, rows)], sems, slot, place))
    return mine, copies


def deal(src, landing, rows, axes, sizes, sems):
    copies = []
    for slot, offset in enumerate(offsets(sizes)):
        place, theirs = group_place(axes, sizes, offset)
        copies.append(send(src.at[rows_at(theirs, rows)], landing.at[slot], sems, slot, place))
    _, mine = group_place(axes, sizes, (0,) * len(axes))
    return mine, copies


def pair_places(axis):
    me = lax.axis_index(axis)
    near = me + 1 - 2 * lax.rem(me, 2)
    return me, near, lax.rem(me + 2, 4), lax.rem(near + 2, 4)


def gather_steps(axes, sizes, src, out, sems):
    rows = src.shape[0]
    if sizes == (4,) and axes == ("clip",):
        (axis,) = axes
        me, near, far, _ = pair_places(axis)
        mine = out.at[rows_at(me, rows)]
        theirs = out.at[rows_at(far, rows)]
        first = send(src, mine, sems, 0, {axis: far})
        second = send(src, mine, sems, 1, {axis: near})
        out[rows_at(me, rows), :] = src[...]
        yield
        first.wait_recv()
        third = send(theirs, theirs, sems, 2, {axis: near})
        yield
        second.wait_recv()
        third.wait_recv()
        finish([first, second, third])
    else:
        mine, copies = spread(src, out, rows, axes, sizes, sems)
        out[rows_at(mine, rows), :] = src[...]
        yield
        for copy in copies:
            copy.wait_recv()
        finish(copies)


def chain_steps(axes, sizes, more_axes, more_sizes, src, out, held, sems, more_sems):
    yield from gather_steps(axes, sizes, src, held, sems)
    yield from gather_steps(more_axes, more_sizes, held, out, more_sems)


def scatter_steps(axes, sizes, src, out, landing, part, sems):
    rows = out.shape[0]
    if sizes == (4,) and axes == ("clip",):
        (axis,) = axes
        me, near, far, near_far = pair_places(axis)
        copies = [
            send(src.at[rows_at(near_far, rows)], landing.at[1], sems, 1, {axis: near}),
            send(src.at[rows_at(near, rows)], landing.at[0], sems, 0, {axis: near}),
        ]
        yield
        copies[0].wait_recv()
        part[...] = (
            src[rows_at(far, rows), :].astype(F32) + landing[1].astype(F32)
        ).astype(part.dtype)
        copies.append(send(part, landing.at[2], sems, 2, {axis: far}))
        yield
        copies[1].wait_recv()
        copies[2].wait_recv()
        total = src[rows_at(me, rows), :].astype(F32) + landing[0].astype(F32)
        out[...] = (total + landing[2].astype(F32)).astype(out.dtype)
        finish(copies)
    else:
        mine, copies = deal(src, landing, rows, axes, sizes, sems)
        yield
        total = src[rows_at(mine, rows), :].astype(F32)
        for slot, copy in enumerate(copies):
            copy.wait_recv()
            total = total + landing[slot].astype(F32)
        out[...] = total.astype(out.dtype)
        finish(copies)


def reduce_steps(axes, sizes, src, out, landing, sems, back_sems):
    rows = landing.shape[1]
    mine, copies = deal(src, landing, rows, axes, sizes, sems)
    yield
    total = src[rows_at(mine, rows), :].astype(F32)
    for slot, copy in enumerate(copies):
        copy.wait_recv()
        total = total + landing[slot].astype(F32)
    block = rows_at(mine, rows)
    out[block, :] = total.astype(out.dtype)
    _, backs = spread(out.at[block], out, rows, axes, sizes, back_sems)
    yield
    for copy in backs:
        copy.wait_recv()
    finish(copies)
    finish(backs)


def reduce_stat_steps(
    axes, sizes, more_axes, more_sizes, src, normed, out, stats,
    landing, part, near_sum, near_held, far_held, sems, back_sems, near_sems, far_sems,
):
    rows = landing.shape[1]
    mine, copies = deal(src, landing, rows, axes, sizes, sems)
    yield
    total = src[rows_at(mine, rows), :].astype(F32)
    for slot, copy in enumerate(copies):
        copy.wait_recv()
        total = total + landing[slot].astype(F32)
    low = total.astype(out.dtype)
    block = rows_at(mine, rows)
    out[block, :] = low
    _, backs = spread(out.at[block], out, rows, axes, sizes, back_sems)
    low = low.astype(F32)
    part[...] = jnp.zeros_like(part)
    part[0:1, :] = jnp.sum(low * normed[...], axis=0, keepdims=True)
    part[1:2, :] = jnp.sum(low, axis=0, keepdims=True)
    yield from share_steps(axes, sizes, part, near_sum, near_held, near_sems)
    yield from share_steps(more_axes, more_sizes, near_sum, stats, far_held, far_sems)
    for copy in backs:
        copy.wait_recv()
    finish(copies)
    finish(backs)


def sum_blocks(held, rows, count):
    total = held[0:rows, :].astype(F32)
    for index in range(1, count):
        total = total + held[index * rows : (index + 1) * rows, :].astype(F32)
    return total


def share_steps(axes, sizes, src, out, held, sems):
    rows = src.shape[0]
    mine, copies = spread(src, held, rows, axes, sizes, sems)
    held[rows_at(mine, rows), :] = src[...]
    yield
    for copy in copies:
        copy.wait_recv()
    out[...] = sum_blocks(held, rows, len(copies) + 1).astype(out.dtype)
    finish(copies)


def both_steps(
    axes, sizes, more_axes, more_sizes, src, out, landing, part, owned, held, sems, more_sems
):
    yield from scatter_steps(axes, sizes, src, owned, landing, part, sems)
    yield from share_steps(more_axes, more_sizes, owned, out, held, more_sems)


def plan_of(kind, axes, sizes, more, array, out_type):
    rows, cols = (array[0] if kind == "reduce_stat" else array).shape
    count = 1
    for size in sizes:
        count *= size
    peers = count - 1
    pair = pltpu.SemaphoreType.DMA((2, peers))
    if kind == "gather":
        return (count * rows, cols), [pair], functools.partial(gather_steps, axes, sizes)
    if kind == "share":
        held = pltpu.VMEM((count * rows, cols), array.dtype)
        return (rows, cols), [held, pair], functools.partial(share_steps, axes, sizes)
    if kind == "chain":
        more_axes, more_sizes = more
        more_count = 1
        for size in more_sizes:
            more_count *= size
        return (
            (more_count * count * rows, cols),
            [
                pltpu.VMEM((count * rows, cols), array.dtype),
                pair,
                pltpu.SemaphoreType.DMA((2, more_count - 1)),
            ],
            functools.partial(chain_steps, axes, sizes, more_axes, more_sizes),
        )
    if kind == "reduce_stat":
        more_axes, more_sizes = more
        more_count = 1
        for size in more_sizes:
            more_count *= size
        small = pltpu.VMEM((8, cols), F32)
        return (
            [(rows, cols), (8, cols)],
            [
                pltpu.VMEM((peers, rows // count, cols), array[0].dtype),
                small,
                small,
                pltpu.VMEM((count * 8, cols), F32),
                pltpu.VMEM((more_count * 8, cols), F32),
                pair,
                pair,
                pair,
                pltpu.SemaphoreType.DMA((2, more_count - 1)),
            ],
            functools.partial(reduce_stat_steps, axes, sizes, more_axes, more_sizes),
        )
    block = rows // count
    one = pltpu.VMEM((block, cols), array.dtype)
    landing = pltpu.VMEM((peers, block, cols), array.dtype)
    if kind == "scatter":
        return (block, cols), [landing, one, pair], functools.partial(scatter_steps, axes, sizes)
    if kind == "reduce":
        return (
            (rows, cols),
            [landing, pair, pair],
            functools.partial(reduce_steps, axes, sizes),
        )
    more_axes, more_sizes = more
    more_count = 1
    for size in more_sizes:
        more_count *= size
    return (
        (block, cols),
        [
            landing,
            one,
            one,
            pltpu.VMEM((more_count * block, cols), array.dtype),
            pair,
            pltpu.SemaphoreType.DMA((2, more_count - 1)),
        ],
        functools.partial(both_steps, axes, sizes, more_axes, more_sizes),
    )


def transfers(collective_id, name, jobs):
    def sized(axes):
        return tuple(lax.axis_size(axis) for axis in axes)

    plans = []
    groups = []
    for job in jobs:
        kind, axes, array, out_type = job[:4]
        more = (job[4], sized(job[4])) if len(job) > 4 else None
        plans.append(plan_of(kind, axes, sized(axes), more, array, out_type))
        for group in (axes,) + ((job[4],) if len(job) > 4 else ()):
            if group not in groups:
                groups.append(group)
    places = {}
    for group in groups:
        for offset in offsets(sized(group)):
            key = tuple(sorted((a, o) for a, o in zip(group, offset) if o))
            places.setdefault(key, (group, offset))
    in_counts = [len(job[2]) if isinstance(job[2], tuple) else 1 for job in jobs]
    arrays = []
    shapes = []
    out_counts = []
    for job, plan in zip(jobs, plans):
        arrays.extend(job[2] if isinstance(job[2], tuple) else (job[2],))
        many = isinstance(plan[0], list)
        outs = zip(plan[0], job[3]) if many else [(plan[0], job[3])]
        outs = [jax.ShapeDtypeStruct(shape, kind) for shape, kind in outs]
        shapes.extend(outs)
        out_counts.append(len(outs))

    def kernel(*refs):
        sources = list(refs[: len(arrays)])
        outs = list(refs[len(arrays) : len(arrays) + len(shapes)])
        scratch = list(refs[len(arrays) + len(shapes) :])
        barrier = pltpu.get_barrier_semaphore()
        for group, offset in places.values():
            place, _ = group_place(group, sized(group), offset)
            pl.semaphore_signal(
                barrier, inc=1, device_id=place, device_id_type=pl.DeviceIdType.MESH
            )
        pl.semaphore_wait(barrier, len(places))
        running = []
        for ins, made, (_, needs, steps) in zip(in_counts, out_counts, plans):
            mine, scratch = scratch[: len(needs)], scratch[len(needs) :]
            running.append(steps(*sources[:ins], *outs[:made], *mine))
            sources, outs = sources[ins:], outs[made:]
        while running:
            running = [step for step in running if next(step, "end") != "end"]

    whole = pl.BlockSpec(memory_space=pltpu.VMEM)
    return pl.pallas_call(
        kernel,
        name=name,
        out_shape=shapes,
        in_specs=[whole] * len(arrays),
        out_specs=[whole] * len(shapes),
        scratch_shapes=[need for plan in plans for need in plan[1]],
        compiler_params=pltpu.CompilerParams(
            collective_id=collective_id,
            has_side_effects=True,
            vmem_limit_bytes=56 * 1024 * 1024,
        ),
    )(*arrays)


def pack_vectors(vectors):
    flat = jnp.concatenate(vectors)
    width = -(-flat.shape[0] // (8 * 128)) * 128
    return jnp.pad(flat, (0, 8 * width - flat.shape[0])).reshape(8, width)


def unpack_vectors(packed, sizes):
    flat = packed.reshape(-1)
    out = []
    at = 0
    for size in sizes:
        out.append(flat[at : at + size])
        at += size
    return out


def shards(
    frames,
    cotangent,
    first_gain,
    first_shift,
    query_weight,
    query_bias,
    key_weight,
    value_weight,
    value_bias,
    out_weight,
    out_bias,
    second_gain,
    second_shift,
    expand_weight,
    expand_bias,
    reduce_weight,
    reduce_bias,
):
    row_count, width = frames.shape
    local_width = query_weight.shape[1]
    head_count = local_width // DH
    score_scale = DH ** (-0.5)
    share = first_gain.shape[0]
    hidden_width = expand_weight.shape[1]
    clips = lax.axis_size("clip")
    clip_at = lax.axis_index("clip") * share
    flat = jnp.concatenate(
        [first_gain, first_shift, out_bias, second_gain, second_shift, reduce_bias]
    )
    wide = -(-flat.shape[0] // (16 * 128)) * 128
    vectors = jnp.pad(flat, (0, 16 * wide - flat.shape[0])).reshape(16, wide)
    attn_weights = jnp.concatenate([query_weight, key_weight, value_weight], axis=1)
    qkv_full, vectors_full, out_blocks, frames_all = transfers(
        1,
        "gather_first",
        [
            ("gather", ("clip",), attn_weights, BF16),
            ("gather", ("clip",), vectors, BF16),
            ("chain", ("tp",), out_weight, BF16, ("clip",)),
            ("gather", ("ctx",), frames, BF16),
        ],
    )
    vectors_full = vectors_full.reshape(clips, 16 * wide)[:, : 6 * share].reshape(clips, 6, share)
    vectors_full = vectors_full.transpose(1, 0, 2).reshape(6, width).astype(F32)
    gain_first, shift_first, out_shift, gain_second, shift_second, reduce_shift = [
        vectors_full[i] for i in range(6)
    ]
    kv_full = qkv_full[:, local_width:]
    query_full = qkv_full[:, :local_width]
    out_blocks = out_blocks.reshape(clips, width, share)
    out_all = out_blocks.transpose(1, 0, 2).reshape(width, width)
    out_rows = lax.dynamic_slice_in_dim(out_all, lax.axis_index("tp") * local_width, local_width)
    inputs = frames.astype(F32)
    normed_one, factor_one = center_rows(inputs)
    first_norm = (normed_one * gain_first + shift_first).astype(BF16)
    queries = (product(first_norm, query_full) + query_bias.astype(F32)).astype(BF16)
    normed_all, _ = center_rows(frames_all.astype(F32))
    norm_all = (normed_all * gain_first + shift_first).astype(BF16)
    kv_bias = jnp.concatenate([jnp.zeros_like(value_bias), value_bias]).astype(F32)
    kv_rows = (product(norm_all, kv_full) + kv_bias).astype(BF16)
    length = kv_rows.shape[0]
    query_heads = queries.reshape(row_count, head_count, DH)
    key_heads = kv_rows[:, :local_width].reshape(length, head_count, DH)
    value_heads = kv_rows[:, local_width:].reshape(length, head_count, DH)
    scores = (
        jnp.einsum("qhd,khd->qhk", query_heads, key_heads, preferred_element_type=F32)
        * score_scale
    )
    run_max = jnp.max(scores, axis=-1)
    weights = jnp.exp(scores - run_max[..., None])
    run_sum = jnp.sum(weights, axis=-1)
    run_acc = jnp.einsum(
        "qhk,khd->qhd", weights.astype(BF16), value_heads, preferred_element_type=F32
    )
    mixed_full = run_acc / run_sum[..., None]
    log_total = run_max + jnp.log(run_sum)
    mixed_low = mixed_full.reshape(row_count, local_width).astype(BF16)
    expand_full, reduce_full_t, mixed_all = transfers(
        2,
        "gather_mixed",
        [
            ("gather", ("clip",), expand_weight, BF16),
            ("gather", ("clip",), reduce_weight.T, BF16),
            ("gather", ("tp",), mixed_low.T, BF16),
        ],
    )
    hidden = inputs + rows_inner(mixed_all, out_all) + out_shift
    normed_two, factor_two = center_rows(hidden)
    second_norm = (normed_two * gain_second + shift_second).astype(BF16)
    pre_act = product(second_norm, expand_full) + expand_bias.astype(F32)

    def gelu_exact(argument):
        return jax.nn.gelu(argument, approximate=False)

    activated, gelu_pull = jax.vjp(gelu_exact, pre_act)
    act_low = activated.astype(BF16)
    grad_act = product(cotangent, reduce_full_t)
    grad_pre = gelu_pull(grad_act)[0].astype(BF16)
    second_terms = cols_inner(grad_pre, expand_full).astype(BF16)
    grad_expand = rows_inner(second_norm, grad_pre).astype(BF16)
    grad_reduce_t = rows_inner(cotangent, act_low).astype(BF16)
    share_expand, share_reduce_t, grad_second = transfers(
        3,
        "grad_second",
        [
            ("scatter", ("clip",), grad_expand, BF16),
            ("scatter", ("clip",), grad_reduce_t, BF16),
            ("reduce", ("tp",), second_terms, BF16),
        ],
    )
    act_late, grad_second = lax.optimization_barrier((act_low, grad_second))
    mlp_terms = cols_inner(act_late, reduce_full_t).astype(BF16)
    tp_size = lax.axis_size("tp")
    tp_at = lax.axis_index("tp")
    part_rows = row_count // tp_size

    def mlp_block(index):
        return lax.dynamic_slice_in_dim(mlp_terms, index * part_rows, part_rows)

    mlp_parts = [mlp_block(tp_at)]
    for step in range(1, tp_size):
        ring = [(i, (i + step) % tp_size) for i in range(tp_size)]
        mlp_parts.append(lax.ppermute(mlp_block((tp_at + step) % tp_size), "tp", ring))
    grad_out = cotangent.astype(F32)
    grad_second = grad_second.astype(F32)
    grad_hidden = grad_out + norm_back(grad_second, normed_two, factor_two, gain_second)
    grad_attn = grad_hidden.astype(BF16)
    grad_out_weight_t = rows_inner(grad_attn, mixed_low).astype(BF16)
    grad_mixed = cols_inner(grad_attn, out_rows).astype(BF16)
    grad_heads = grad_mixed.reshape(row_count, head_count, DH)
    row_delta = jnp.sum(grad_heads.astype(F32) * mixed_full, axis=-1)
    weights_low, grad_scores = score_block(
        query_heads, key_heads, value_heads, grad_heads, log_total, row_delta, score_scale
    )
    grad_query = jnp.einsum("qhk,khd->qhd", grad_scores, key_heads, preferred_element_type=F32)
    key_term = jnp.einsum("qhk,qhd->khd", grad_scores, query_heads, preferred_element_type=F32)
    value_term = jnp.einsum("qhk,qhd->khd", weights_low, grad_heads, preferred_element_type=F32)
    kv_terms = jnp.concatenate(
        [
            (key_term * score_scale).reshape(length, local_width),
            value_term.reshape(length, local_width),
        ],
        axis=1,
    ).astype(BF16)
    mlp_part = mlp_parts[0].astype(F32)
    for part in mlp_parts[1:]:
        mlp_part = mlp_part + part.astype(F32)
    grad_kv_low, mlp_sum = transfers(
        4,
        "grad_kv",
        [
            ("scatter", ("ctx",), kv_terms, BF16),
            ("gather", ("tp",), mlp_part.astype(BF16), BF16),
        ],
    )
    layer_out = (hidden + mlp_sum.astype(F32) + reduce_shift).astype(BF16)
    grad_q_low = (grad_query * score_scale).reshape(row_count, local_width).astype(BF16)
    grad_qkv = jnp.concatenate([grad_q_low, grad_kv_low], axis=1)
    first_terms = cols_inner(grad_qkv, qkv_full).astype(BF16)
    grad_attn_weights = jnp.concatenate(
        [rows_inner(first_norm, grad_qkv).astype(BF16), grad_out_weight_t], axis=1
    )
    qkv_bias = jnp.sum(grad_qkv.astype(F32), axis=0)
    early = [
        jnp.sum(grad_out, axis=0),
        jnp.sum(grad_second * normed_two, axis=0),
        jnp.sum(grad_second, axis=0),
        jnp.sum(grad_attn.astype(F32), axis=0),
        jnp.sum(grad_pre.astype(F32), axis=0),
        qkv_bias[:local_width],
        qkv_bias[2 * local_width :],
    ]
    normed_part = lax.dynamic_slice_in_dim(normed_one, tp_at * part_rows, part_rows)
    sum_attn, grad_first, late_sum, sum_expand, sum_reduce_t, early_sum = transfers(
        5,
        "grad_first",
        [
            ("both", ("clip",), grad_attn_weights, F32, ("ctx",)),
            (
                "reduce_stat",
                ("tp",),
                (first_terms, normed_part),
                (BF16, F32),
                ("clip", "ctx"),
            ),
            ("share", ("ctx",), share_expand, F32),
            ("share", ("ctx",), share_reduce_t, F32),
            ("share", ("clip", "ctx"), pack_vectors(early), F32),
        ],
    )
    grad_first = grad_first.astype(F32)
    frames_grad = grad_hidden + norm_back(grad_first, normed_one, factor_one, gain_first)

    sums = unpack_vectors(early_sum, [4 * width, hidden_width, local_width, local_width])
    shared = jnp.concatenate([sums[0].reshape(4, width), late_sum[:2]])
    shared = lax.dynamic_slice(shared, (0, clip_at), (6, share))
    return (
        layer_out,
        frames_grad,
        shared[4],
        shared[5],
        sum_attn[:, :local_width],
        sums[2],
        sum_attn[:, local_width : 2 * local_width],
        sum_attn[:, 2 * local_width : 3 * local_width],
        sums[3],
        sum_attn[:, 3 * local_width :].T,
        shared[3],
        shared[1],
        shared[2],
        sum_expand,
        sums[1],
        sum_reduce_t.T,
        shared[0],
    )


def solution(mesh):
    placed = (
        P(("clip", "ctx"), None),
        P(("clip", "ctx"), None),
        P("clip"),
        P("clip"),
        P("clip", "tp"),
        P("tp"),
        P("clip", "tp"),
        P("clip", "tp"),
        P("tp"),
        P("tp", "clip"),
        P("clip"),
        P("clip"),
        P("clip"),
        P("clip", "tp"),
        P("tp"),
        P("tp", "clip"),
        P("clip"),
    )
    return jax.shard_map(
        shards,
        mesh=mesh,
        in_specs=placed,
        out_specs=(
            P(("clip", "ctx"), None),
            P(("clip", "ctx"), None),
            P("clip"),
            P("clip"),
            P("clip", "tp"),
            P("tp"),
            P("clip", "tp"),
            P("clip", "tp"),
            P("tp"),
            P("tp", "clip"),
            P("clip"),
            P("clip"),
            P("clip"),
            P("clip", "tp"),
            P("tp"),
            P("tp", "clip"),
            P("clip"),
        ),
        check_vma=False,
    )
```

```python
import functools
import itertools

import jax
import jax.numpy as jnp
from jax import lax
from jax.experimental import pallas as pl
from jax.experimental.pallas import tpu as pltpu
from jax.sharding import PartitionSpec as P

DH = 64


def center_rows(matrix):
    row_mean = jnp.mean(matrix, axis=-1, keepdims=True)
    centred = matrix - row_mean
    factor = lax.rsqrt(jnp.mean(centred * centred, axis=-1, keepdims=True) + 1e-05)
    return (centred * factor, factor)


def norm_back(grad_norm, normed, factor, gain):
    grad_hat = grad_norm * gain
    inner = jnp.mean(grad_hat, axis=-1, keepdims=True)
    cross = jnp.mean(grad_hat * normed, axis=-1, keepdims=True)
    return factor * (grad_hat - inner - normed * cross)


def product(left, right):
    return jnp.dot(left, right, preferred_element_type=jnp.float32)


def rows_inner(left, right):
    return lax.dot_general(
        left, right, (((0,), (0,)), ((), ())), preferred_element_type=jnp.float32
    )


def cols_inner(left, right):
    return lax.dot_general(
        left, right, (((1,), (1,)), ((), ())), preferred_element_type=jnp.float32
    )


def score_block(query_heads, key_heads, value_heads, grad_heads, log_total, row_delta, score_scale):
    scores = (
        jnp.einsum("qhd,khd->qhk", query_heads, key_heads, preferred_element_type=jnp.float32)
        * score_scale
    )
    weights = jnp.exp(scores - log_total[..., None])
    grad_weights = jnp.einsum(
        "qhd,khd->qhk", grad_heads, value_heads, preferred_element_type=jnp.float32
    )
    grad_scores = (weights * (grad_weights - row_delta[..., None])).astype(jnp.bfloat16)
    return (weights.astype(jnp.bfloat16), grad_scores)


F32 = jnp.float32
BF16 = jnp.bfloat16


def offsets(sizes):
    return [o for o in itertools.product(*(range(s) for s in sizes)) if any(o)]


def group_place(axes, sizes, offset):
    index = 0
    place = {}
    for axis, size, step in zip(axes, sizes, offset):
        at = lax.rem(lax.axis_index(axis) + step, size)
        place[axis] = at
        index = index * size + at
    return place, index


def rows_at(index, rows):
    return pl.ds(pl.multiple_of(index * rows, rows), rows)


def send(src, dst, sems, slot, place):
    copy = pltpu.make_async_remote_copy(
        src_ref=src,
        dst_ref=dst,
        send_sem=sems.at[0, slot],
        recv_sem=sems.at[1, slot],
        device_id=place,
        device_id_type=pl.DeviceIdType.MESH,
    )
    copy.start()
    return copy


def finish(copies):
    for copy in copies:
        copy.wait_send()


def spread(src, dst, rows, axes, sizes, sems):
    _, mine = group_place(axes, sizes, (0,) * len(axes))
    copies = []
    for slot, offset in enumerate(offsets(sizes)):
        place, _ = group_place(axes, sizes, offset)
        copies.append(send(src, dst.at[rows_at(mine, rows)], sems, slot, place))
    return mine, copies


def deal(src, landing, rows, axes, sizes, sems):
    copies = []
    for slot, offset in enumerate(offsets(sizes)):
        place, theirs = group_place(axes, sizes, offset)
        copies.append(send(src.at[rows_at(theirs, rows)], landing.at[slot], sems, slot, place))
    _, mine = group_place(axes, sizes, (0,) * len(axes))
    return mine, copies


def pair_places(axis):
    me = lax.axis_index(axis)
    near = me + 1 - 2 * lax.rem(me, 2)
    return me, near, lax.rem(me + 2, 4), lax.rem(near + 2, 4)


def gather_steps(axes, sizes, src, out, sems):
    rows = src.shape[0]
    if sizes == (4,) and axes == ("clip",):
        (axis,) = axes
        me, near, far, _ = pair_places(axis)
        mine = out.at[rows_at(me, rows)]
        theirs = out.at[rows_at(far, rows)]
        first = send(src, mine, sems, 0, {axis: far})
        second = send(src, mine, sems, 1, {axis: near})
        out[rows_at(me, rows), :] = src[...]
        yield
        first.wait_recv()
        third = send(theirs, theirs, sems, 2, {axis: near})
        yield
        second.wait_recv()
        third.wait_recv()
        finish([first, second, third])
    else:
        mine, copies = spread(src, out, rows, axes, sizes, sems)
        out[rows_at(mine, rows), :] = src[...]
        yield
        for copy in copies:
            copy.wait_recv()
        finish(copies)


def chain_steps(axes, sizes, more_axes, more_sizes, src, out, held, sems, more_sems):
    yield from gather_steps(axes, sizes, src, held, sems)
    yield from gather_steps(more_axes, more_sizes, held, out, more_sems)


def scatter_steps(axes, sizes, src, out, landing, part, sems):
    rows = out.shape[0]
    if sizes == (4,) and axes == ("clip",):
        (axis,) = axes
        me, near, far, near_far = pair_places(axis)
        copies = [
            send(src.at[rows_at(near_far, rows)], landing.at[1], sems, 1, {axis: near}),
            send(src.at[rows_at(near, rows)], landing.at[0], sems, 0, {axis: near}),
        ]
        yield
        copies[0].wait_recv()
        part[...] = (
            src[rows_at(far, rows), :].astype(F32) + landing[1].astype(F32)
        ).astype(part.dtype)
        copies.append(send(part, landing.at[2], sems, 2, {axis: far}))
        yield
        copies[1].wait_recv()
        copies[2].wait_recv()
        total = src[rows_at(me, rows), :].astype(F32) + landing[0].astype(F32)
        out[...] = (total + landing[2].astype(F32)).astype(out.dtype)
        finish(copies)
    else:
        mine, copies = deal(src, landing, rows, axes, sizes, sems)
        yield
        total = src[rows_at(mine, rows), :].astype(F32)
        for slot, copy in enumerate(copies):
            copy.wait_recv()
            total = total + landing[slot].astype(F32)
        out[...] = total.astype(out.dtype)
        finish(copies)


def reduce_steps(axes, sizes, src, out, landing, sems, back_sems):
    rows = landing.shape[1]
    mine, copies = deal(src, landing, rows, axes, sizes, sems)
    yield
    total = src[rows_at(mine, rows), :].astype(F32)
    for slot, copy in enumerate(copies):
        copy.wait_recv()
        total = total + landing[slot].astype(F32)
    block = rows_at(mine, rows)
    out[block, :] = total.astype(out.dtype)
    _, backs = spread(out.at[block], out, rows, axes, sizes, back_sems)
    yield
    for copy in backs:
        copy.wait_recv()
    finish(copies)
    finish(backs)


def reduce_stat_steps(
    axes, sizes, more_axes, more_sizes, src, normed, out, stats,
    landing, part, near_sum, near_held, far_held, sems, back_sems, near_sems, far_sems,
):
    rows = landing.shape[1]
    mine, copies = deal(src, landing, rows, axes, sizes, sems)
    yield
    total = src[rows_at(mine, rows), :].astype(F32)
    for slot, copy in enumerate(copies):
        copy.wait_recv()
        total = total + landing[slot].astype(F32)
    block = rows_at(mine, rows)
    out[block, :] = total.astype(out.dtype)
    low = out[block, :].astype(F32)
    part[...] = jnp.zeros_like(part)
    part[0:1, :] = jnp.sum(low * normed[...], axis=0, keepdims=True)
    part[1:2, :] = jnp.sum(low, axis=0, keepdims=True)
    near = share_steps(axes, sizes, part, near_sum, near_held, near_sems)
    next(near)
    _, backs = spread(out.at[block], out, rows, axes, sizes, back_sems)
    yield
    next(near, None)
    yield from share_steps(more_axes, more_sizes, near_sum, stats, far_held, far_sems)
    for copy in backs:
        copy.wait_recv()
    finish(copies)
    finish(backs)


def sum_blocks(held, rows, count):
    total = held[0:rows, :].astype(F32)
    for index in range(1, count):
        total = total + held[index * rows : (index + 1) * rows, :].astype(F32)
    return total


def share_steps(axes, sizes, src, out, held, sems):
    rows = src.shape[0]
    mine, copies = spread(src, held, rows, axes, sizes, sems)
    held[rows_at(mine, rows), :] = src[...]
    yield
    for copy in copies:
        copy.wait_recv()
    out[...] = sum_blocks(held, rows, len(copies) + 1).astype(out.dtype)
    finish(copies)


def both_steps(
    axes, sizes, more_axes, more_sizes, src, out, landing, part, owned, held, sems, more_sems
):
    yield from scatter_steps(axes, sizes, src, owned, landing, part, sems)
    yield from share_steps(more_axes, more_sizes, owned, out, held, more_sems)


def plan_of(kind, axes, sizes, more, array, out_type):
    rows, cols = (array[0] if kind == "reduce_stat" else array).shape
    count = 1
    for size in sizes:
        count *= size
    peers = count - 1
    pair = pltpu.SemaphoreType.DMA((2, peers))
    if kind == "gather":
        return (count * rows, cols), [pair], functools.partial(gather_steps, axes, sizes)
    if kind == "share":
        held = pltpu.VMEM((count * rows, cols), array.dtype)
        return (rows, cols), [held, pair], functools.partial(share_steps, axes, sizes)
    if kind == "chain":
        more_axes, more_sizes = more
        more_count = 1
        for size in more_sizes:
            more_count *= size
        return (
            (more_count * count * rows, cols),
            [
                pltpu.VMEM((count * rows, cols), array.dtype),
                pair,
                pltpu.SemaphoreType.DMA((2, more_count - 1)),
            ],
            functools.partial(chain_steps, axes, sizes, more_axes, more_sizes),
        )
    if kind == "reduce_stat":
        more_axes, more_sizes = more
        more_count = 1
        for size in more_sizes:
            more_count *= size
        small = pltpu.VMEM((8, cols), F32)
        return (
            [(rows, cols), (8, cols)],
            [
                pltpu.VMEM((peers, rows // count, cols), array[0].dtype),
                small,
                small,
                pltpu.VMEM((count * 8, cols), F32),
                pltpu.VMEM((more_count * 8, cols), F32),
                pair,
                pair,
                pair,
                pltpu.SemaphoreType.DMA((2, more_count - 1)),
            ],
            functools.partial(reduce_stat_steps, axes, sizes, more_axes, more_sizes),
        )
    block = rows // count
    one = pltpu.VMEM((block, cols), array.dtype)
    landing = pltpu.VMEM((peers, block, cols), array.dtype)
    if kind == "scatter":
        return (block, cols), [landing, one, pair], functools.partial(scatter_steps, axes, sizes)
    if kind == "reduce":
        return (
            (rows, cols),
            [landing, pair, pair],
            functools.partial(reduce_steps, axes, sizes),
        )
    more_axes, more_sizes = more
    more_count = 1
    for size in more_sizes:
        more_count *= size
    return (
        (block, cols),
        [
            landing,
            one,
            one,
            pltpu.VMEM((more_count * block, cols), array.dtype),
            pair,
            pltpu.SemaphoreType.DMA((2, more_count - 1)),
        ],
        functools.partial(both_steps, axes, sizes, more_axes, more_sizes),
    )


def transfers(collective_id, name, jobs):
    def sized(axes):
        return tuple(lax.axis_size(axis) for axis in axes)

    plans = []
    groups = []
    for job in jobs:
        kind, axes, array, out_type = job[:4]
        more = (job[4], sized(job[4])) if len(job) > 4 else None
        plans.append(plan_of(kind, axes, sized(axes), more, array, out_type))
        for group in (axes,) + ((job[4],) if len(job) > 4 else ()):
            if group not in groups:
                groups.append(group)
    places = {}
    for group in groups:
        for offset in offsets(sized(group)):
            key = tuple(sorted((a, o) for a, o in zip(group, offset) if o))
            places.setdefault(key, (group, offset))
    in_counts = [len(job[2]) if isinstance(job[2], tuple) else 1 for job in jobs]
    arrays = []
    shapes = []
    out_counts = []
    for job, plan in zip(jobs, plans):
        arrays.extend(job[2] if isinstance(job[2], tuple) else (job[2],))
        many = isinstance(plan[0], list)
        outs = zip(plan[0], job[3]) if many else [(plan[0], job[3])]
        outs = [jax.ShapeDtypeStruct(shape, kind) for shape, kind in outs]
        shapes.extend(outs)
        out_counts.append(len(outs))

    def kernel(*refs):
        sources = list(refs[: len(arrays)])
        outs = list(refs[len(arrays) : len(arrays) + len(shapes)])
        scratch = list(refs[len(arrays) + len(shapes) :])
        barrier = pltpu.get_barrier_semaphore()
        for group, offset in places.values():
            place, _ = group_place(group, sized(group), offset)
            pl.semaphore_signal(
                barrier, inc=1, device_id=place, device_id_type=pl.DeviceIdType.MESH
            )
        pl.semaphore_wait(barrier, len(places))
        running = []
        for ins, made, (_, needs, steps) in zip(in_counts, out_counts, plans):
            mine, scratch = scratch[: len(needs)], scratch[len(needs) :]
            running.append(steps(*sources[:ins], *outs[:made], *mine))
            sources, outs = sources[ins:], outs[made:]
        while running:
            running = [step for step in running if next(step, "end") != "end"]

    whole = pl.BlockSpec(memory_space=pltpu.VMEM)
    return pl.pallas_call(
        kernel,
        name=name,
        out_shape=shapes,
        in_specs=[whole] * len(arrays),
        out_specs=[whole] * len(shapes),
        scratch_shapes=[need for plan in plans for need in plan[1]],
        compiler_params=pltpu.CompilerParams(
            collective_id=collective_id,
            has_side_effects=True,
            vmem_limit_bytes=56 * 1024 * 1024,
        ),
    )(*arrays)


def pack_vectors(vectors):
    flat = jnp.concatenate(vectors)
    width = -(-flat.shape[0] // (8 * 128)) * 128
    return jnp.pad(flat, (0, 8 * width - flat.shape[0])).reshape(8, width)


def unpack_vectors(packed, sizes):
    flat = packed.reshape(-1)
    out = []
    at = 0
    for size in sizes:
        out.append(flat[at : at + size])
        at += size
    return out


def shards(
    frames,
    cotangent,
    first_gain,
    first_shift,
    query_weight,
    query_bias,
    key_weight,
    value_weight,
    value_bias,
    out_weight,
    out_bias,
    second_gain,
    second_shift,
    expand_weight,
    expand_bias,
    reduce_weight,
    reduce_bias,
):
    row_count, width = frames.shape
    local_width = query_weight.shape[1]
    head_count = local_width // DH
    score_scale = DH ** (-0.5)
    share = first_gain.shape[0]
    hidden_width = expand_weight.shape[1]
    clips = lax.axis_size("clip")
    clip_at = lax.axis_index("clip") * share
    flat = jnp.concatenate(
        [first_gain, first_shift, out_bias, second_gain, second_shift, reduce_bias]
    )
    wide = -(-flat.shape[0] // (16 * 128)) * 128
    vectors = jnp.pad(flat, (0, 16 * wide - flat.shape[0])).reshape(16, wide)
    attn_weights = jnp.concatenate([query_weight, key_weight, value_weight], axis=1)
    qkv_full, vectors_full, out_blocks, frames_all = transfers(
        1,
        "gather_first",
        [
            ("gather", ("clip",), attn_weights, BF16),
            ("gather", ("clip",), vectors, BF16),
            ("chain", ("tp",), out_weight, BF16, ("clip",)),
            ("gather", ("ctx",), frames, BF16),
        ],
    )
    vectors_full = vectors_full.reshape(clips, 16 * wide)[:, : 6 * share].reshape(clips, 6, share)
    vectors_full = vectors_full.transpose(1, 0, 2).reshape(6, width).astype(F32)
    gain_first, shift_first, out_shift, gain_second, shift_second, reduce_shift = [
        vectors_full[i] for i in range(6)
    ]
    kv_full = qkv_full[:, local_width:]
    query_full = qkv_full[:, :local_width]
    out_blocks = out_blocks.reshape(clips, width, share)
    out_all = out_blocks.transpose(1, 0, 2).reshape(width, width)
    out_rows = lax.dynamic_slice_in_dim(out_all, lax.axis_index("tp") * local_width, local_width)
    inputs = frames.astype(F32)
    normed_one, factor_one = center_rows(inputs)
    first_norm = (normed_one * gain_first + shift_first).astype(BF16)
    queries = (product(first_norm, query_full) + query_bias.astype(F32)).astype(BF16)
    normed_all, _ = center_rows(frames_all.astype(F32))
    norm_all = (normed_all * gain_first + shift_first).astype(BF16)
    kv_bias = jnp.concatenate([jnp.zeros_like(value_bias), value_bias]).astype(F32)
    kv_rows = (product(norm_all, kv_full) + kv_bias).astype(BF16)
    length = kv_rows.shape[0]
    query_heads = queries.reshape(row_count, head_count, DH)
    key_heads = kv_rows[:, :local_width].reshape(length, head_count, DH)
    value_heads = kv_rows[:, local_width:].reshape(length, head_count, DH)
    scores = (
        jnp.einsum("qhd,khd->qhk", query_heads, key_heads, preferred_element_type=F32)
        * score_scale
    )
    run_max = jnp.max(scores, axis=-1)
    weights = jnp.exp(scores - run_max[..., None])
    run_sum = jnp.sum(weights, axis=-1)
    run_acc = jnp.einsum(
        "qhk,khd->qhd", weights.astype(BF16), value_heads, preferred_element_type=F32
    )
    mixed_full = run_acc / run_sum[..., None]
    log_total = run_max + jnp.log(run_sum)
    mixed_low = mixed_full.reshape(row_count, local_width).astype(BF16)
    expand_full, reduce_full_t, mixed_all = transfers(
        2,
        "gather_mixed",
        [
            ("gather", ("clip",), expand_weight, BF16),
            ("gather", ("clip",), reduce_weight.T, BF16),
            ("gather", ("tp",), mixed_low.T, BF16),
        ],
    )
    hidden = inputs + rows_inner(mixed_all, out_all) + out_shift
    normed_two, factor_two = center_rows(hidden)
    second_norm = (normed_two * gain_second + shift_second).astype(BF16)
    pre_act = product(second_norm, expand_full) + expand_bias.astype(F32)

    def gelu_exact(argument):
        return jax.nn.gelu(argument, approximate=False)

    activated, gelu_pull = jax.vjp(gelu_exact, pre_act)
    act_low = activated.astype(BF16)
    grad_act = product(cotangent, reduce_full_t)
    grad_pre = gelu_pull(grad_act)[0].astype(BF16)
    second_terms = cols_inner(grad_pre, expand_full).astype(BF16)
    grad_expand = rows_inner(second_norm, grad_pre).astype(BF16)
    grad_reduce_t = rows_inner(cotangent, act_low).astype(BF16)
    share_expand, share_reduce_t, grad_second = transfers(
        3,
        "grad_second",
        [
            ("scatter", ("clip",), grad_expand, BF16),
            ("scatter", ("clip",), grad_reduce_t, BF16),
            ("reduce", ("tp",), second_terms, BF16),
        ],
    )
    act_late, grad_second = lax.optimization_barrier((act_low, grad_second))
    mlp_terms = cols_inner(act_late, reduce_full_t).astype(BF16)
    tp_size = lax.axis_size("tp")
    tp_at = lax.axis_index("tp")
    part_rows = row_count // tp_size

    def mlp_block(index):
        return lax.dynamic_slice_in_dim(mlp_terms, index * part_rows, part_rows)

    mlp_parts = [mlp_block(tp_at)]
    for step in range(1, tp_size):
        ring = [(i, (i + step) % tp_size) for i in range(tp_size)]
        mlp_parts.append(lax.ppermute(mlp_block((tp_at + step) % tp_size), "tp", ring))
    grad_out = cotangent.astype(F32)
    grad_second = grad_second.astype(F32)
    grad_hidden = grad_out + norm_back(grad_second, normed_two, factor_two, gain_second)
    grad_attn = grad_hidden.astype(BF16)
    grad_out_weight_t = rows_inner(grad_attn, mixed_low).astype(BF16)
    grad_mixed = cols_inner(grad_attn, out_rows).astype(BF16)
    grad_heads = grad_mixed.reshape(row_count, head_count, DH)
    row_delta = jnp.sum(grad_heads.astype(F32) * mixed_full, axis=-1)
    weights_low, grad_scores = score_block(
        query_heads, key_heads, value_heads, grad_heads, log_total, row_delta, score_scale
    )
    grad_query = jnp.einsum("qhk,khd->qhd", grad_scores, key_heads, preferred_element_type=F32)
    key_term = jnp.einsum("qhk,qhd->khd", grad_scores, query_heads, preferred_element_type=F32)
    value_term = jnp.einsum("qhk,qhd->khd", weights_low, grad_heads, preferred_element_type=F32)
    kv_terms = jnp.concatenate(
        [
            (key_term * score_scale).reshape(length, local_width),
            value_term.reshape(length, local_width),
        ],
        axis=1,
    ).astype(BF16)
    mlp_part = mlp_parts[0].astype(F32)
    for part in mlp_parts[1:]:
        mlp_part = mlp_part + part.astype(F32)
    grad_kv_low, mlp_sum = transfers(
        4,
        "grad_kv",
        [
            ("scatter", ("ctx",), kv_terms, BF16),
            ("gather", ("tp",), mlp_part.astype(BF16), BF16),
        ],
    )
    layer_out = (hidden + mlp_sum.astype(F32) + reduce_shift).astype(BF16)
    grad_q_low = (grad_query * score_scale).reshape(row_count, local_width).astype(BF16)
    grad_qkv = jnp.concatenate([grad_q_low, grad_kv_low], axis=1)
    first_terms = cols_inner(grad_qkv, qkv_full).astype(BF16)
    grad_attn_weights = jnp.concatenate(
        [rows_inner(first_norm, grad_qkv).astype(BF16), grad_out_weight_t], axis=1
    )
    qkv_bias = jnp.sum(grad_qkv.astype(F32), axis=0)
    early = [
        jnp.sum(grad_out, axis=0),
        jnp.sum(grad_second * normed_two, axis=0),
        jnp.sum(grad_second, axis=0),
        jnp.sum(grad_attn.astype(F32), axis=0),
        jnp.sum(grad_pre.astype(F32), axis=0),
        qkv_bias[:local_width],
        qkv_bias[2 * local_width :],
    ]
    normed_part = lax.dynamic_slice_in_dim(normed_one, tp_at * part_rows, part_rows)
    sum_attn, grad_first, late_sum, sum_expand, sum_reduce_t, early_sum = transfers(
        5,
        "grad_first",
        [
            ("both", ("clip",), grad_attn_weights, F32, ("ctx",)),
            (
                "reduce_stat",
                ("tp",),
                (first_terms, normed_part),
                (BF16, F32),
                ("clip", "ctx"),
            ),
            ("share", ("ctx",), share_expand, F32),
            ("share", ("ctx",), share_reduce_t, F32),
            ("share", ("clip", "ctx"), pack_vectors(early), F32),
        ],
    )
    grad_first = grad_first.astype(F32)
    frames_grad = grad_hidden + norm_back(grad_first, normed_one, factor_one, gain_first)

    sums = unpack_vectors(early_sum, [4 * width, hidden_width, local_width, local_width])
    shared = jnp.concatenate([sums[0].reshape(4, width), late_sum[:2]])
    shared = lax.dynamic_slice(shared, (0, clip_at), (6, share))
    return (
        layer_out,
        frames_grad,
        shared[4],
        shared[5],
        sum_attn[:, :local_width],
        sums[2],
        sum_attn[:, local_width : 2 * local_width],
        sum_attn[:, 2 * local_width : 3 * local_width],
        sums[3],
        sum_attn[:, 3 * local_width :].T,
        shared[3],
        shared[1],
        shared[2],
        sum_expand,
        sums[1],
        sum_reduce_t.T,
        shared[0],
    )


def solution(mesh):
    placed = (
        P(("clip", "ctx"), None),
        P(("clip", "ctx"), None),
        P("clip"),
        P("clip"),
        P("clip", "tp"),
        P("tp"),
        P("clip", "tp"),
        P("clip", "tp"),
        P("tp"),
        P("tp", "clip"),
        P("clip"),
        P("clip"),
        P("clip"),
        P("clip", "tp"),
        P("tp"),
        P("tp", "clip"),
        P("clip"),
    )
    return jax.shard_map(
        shards,
        mesh=mesh,
        in_specs=placed,
        out_specs=(
            P(("clip", "ctx"), None),
            P(("clip", "ctx"), None),
            P("clip"),
            P("clip"),
            P("clip", "tp"),
            P("tp"),
            P("clip", "tp"),
            P("clip", "tp"),
            P("tp"),
            P("tp", "clip"),
            P("clip"),
            P("clip"),
            P("clip"),
            P("clip", "tp"),
            P("tp"),
            P("tp", "clip"),
            P("clip"),
        ),
        check_vma=False,
    )
```
